128 devices in a mesh: grp: 16 (over x, y), rep: 8 (over z, core).
Axes of the slice: x: 4, y: 4, z: 4, core: 2. Of those that a mesh axis runs over, the one named last changes fastest.
Arguments:
- tokens: bfloat16 [4096, 4096], P(('rep', 'grp')), parts along dimension 0, may hold values from -6 to 6
- queries: bfloat16 [4096, 4096], P(('rep', 'grp')), parts along dimension 0, may hold values from -16 to 16
- fresh_kv: bfloat16 [4096, 1024], P(('rep', 'grp')), parts along dimension 0, may hold values from -16 to 16
- old_cache: bfloat16 [4096, 32, 1024], P(('rep', 'grp')), parts along dimension 0, may hold values from -16 to 16
- old_slot: int32 [4096], P(('rep', 'grp')), parts along dimension 0, may hold values from 0 to 31, as said below
- new_owner: int32 [4096, 1], P(('rep', 'grp')), parts along dimension 0, may hold values from 0 to 15; in each aligned block of 32 rows (0 to 31, 32 to 63, ...) at most 4 rows name the same one
- lengths: int32 [4096], P(('rep', 'grp')), parts along dimension 0, may hold values from 1 to 31
- norm_gain: bfloat16 [32768], P('rep'), parts along dimension 0, may hold values from 0.099609375 to 1.8984375
- gate_weight: bfloat16 [32768, 14336], P('rep', 'grp'), parts along dimension 0, may hold values from -0.09375 to 0.09375
- up_weight: bfloat16 [32768, 14336], P('rep', 'grp'), parts along dimension 0, may hold values from -0.09375 to 0.09375
- down_weight: bfloat16 [114688, 4096], P(('rep', 'grp')), parts along dimension 0, may hold values from -0.046875 to 0.046875
Outputs:
- layer_out: bfloat16 [4096, 4096], P(('rep', 'grp')), parts along dimension 0
- new_cache: bfloat16 [8192, 32, 1024], P(('rep', 'grp')), parts along dimension 0
The draws below stay inside these ranges and needn't reach their ends.
There are 8 independent parts, one for each index of `rep`. The reference program is written for one: setup_inputs(seed, part) draws one part's arguments, and reference() takes and returns one part's arrays. A program takes and returns all parts, laid end to end along the dimension named above; each array names one. Nothing has to cross between parts.
Inputs may be any that keep to these rules, and one draw needn't show every extreme that they name: `old_slot`: within each aligned block of 32 requests each slot number appears once. `new_owner`: among the rows of one member (aligned blocks of 32) no new member is named more than 4 times, and some new member is named exactly 4 times.
All inputs are finite; a program needn't handle non-finite values.
Results may differ from the reference program's by a relative error of at most 0.017.
Values may be sent and summed in bfloat16 or wider, within the bound.
A program may use at most 128 MiB of HBM per device.

```python
import math
import jax
import jax.numpy as jnp
import numpy as np
from jax import lax

D = 4096
QH = 32
KVH = 4
HD = 128
FF = 14336
REQ_DEV = 32
CACHE = 32
PER_PEER = 4
REQS = 512
SLOTS = 64
N_GRP = 16


def draw_queries(key, part):
    key = jax.random.fold_in(key, 11)
    result = jnp.clip(jax.random.normal(key, (REQS, QH * HD), jnp.float32), -6.0, 6.0)
    return result.astype(jnp.bfloat16)


def draw_fresh_kv(key, part):
    key = jax.random.fold_in(key, 12)
    result = jnp.clip(jax.random.normal(key, (REQS, 2 * KVH * HD), jnp.float32), -6.0, 6.0)
    return result.astype(jnp.bfloat16)


def draw_old_cache(key, part):
    key = jax.random.fold_in(key, 13)
    result = jnp.clip(jax.random.normal(key, (REQS, CACHE, 2 * KVH * HD), jnp.float32), -6.0, 6.0)
    return result.astype(jnp.bfloat16)


def draw_old_slot(key, part):
    key = jax.random.fold_in(key, 14)
    block_keys = jax.random.split(key, REQS // REQ_DEV)
    orders = jax.vmap(lambda block_key: jax.random.permutation(block_key, REQ_DEV))(block_keys)
    return orders.reshape(REQS).astype(jnp.int32)


def draw_lengths(key, part):
    key = jax.random.fold_in(key, 15)
    values = jax.random.randint(key, (REQS,), 1, CACHE)
    chosen = jax.random.randint(jax.random.fold_in(key, 1), (), 0, REQS)
    return values.at[chosen].set(CACHE - 1).astype(jnp.int32)


def shard_levels(stream_key, shape, cuts, smallest, high):
    factor_of, own = 1.0, jax.random.fold_in(stream_key, 6)
    for axis_at, shards_of in cuts:
        steps = jnp.exp(jax.random.uniform(jax.random.fold_in(own, axis_at), (shards_of,), jnp.float32, smallest / len(cuts), high / len(cuts)))
        factor_of = factor_of * jnp.repeat(steps, shape[axis_at] // shards_of).reshape([-1 if axis == axis_at else 1 for axis in range(len(shape))])
    return factor_of


def shared_out(key, own, number, rows, count, top, limit, slope):
    ranking = jax.random.permutation(key, count)
    heavy_load, common = portions_of(count, rows * top, limit, slope, True), portions_of(count, rows * top, limit, slope, False)
    places = jnp.arange(count)

    def named(sizes, offset_by):
        used = int((sizes > 0).sum())
        fixed = max(1, used // 4)
        moved = fixed + (places - fixed + offset_by * (used - fixed)) % max(1, count - fixed)
        return jnp.zeros((count,), jnp.int32).at[ranking[jnp.where(places < fixed, places, moved)]].set(jnp.asarray(sizes, jnp.int32))

    sizes = jnp.where(number % 4 == 0, named(heavy_load, number // 4), named(common, number - number // 4 - 1))
    mixed = jax.random.permutation(jax.random.fold_in(own, 3), count)
    giver, taker = mixed[0:count // 2 * 2:2], mixed[1:count // 2 * 2:2]
    margin = jnp.minimum(sizes[giver] - 1, limit - sizes[taker]) // 2
    margin = jnp.where((giver == ranking[0]) | (taker == ranking[0]) | (sizes[taker] == 0), 0, jnp.maximum(margin, 0))
    moved = jax.random.randint(jax.random.fold_in(own, 4), (count // 2,), 0, 1 << 20) % (margin + 1)
    sizes = sizes.at[giver].add(-moved).at[taker].add(moved)
    items = jnp.searchsorted(jnp.cumsum(sizes), jnp.arange(rows * top), side="right").astype(jnp.int32)
    listing = items.reshape(top, rows).T
    listing = listing[jax.random.permutation(jax.random.fold_in(own, 1), rows)]
    offset_by = jax.random.randint(jax.random.fold_in(own, 2), (rows, 1), 0, top)
    return jnp.take_along_axis(listing, (jnp.arange(top)[None, :] + offset_by) % top, axis=1)


def portions_of(amount, total, bound, skew, full):
    weights = [(1 << 20) // math.isqrt(rank ** skew) + 1 for rank in range(1, amount + 1)]
    largest = bound if full else min(bound, max(-(-total // amount), total * weights[0] // sum(weights)))
    least = 1 if total - largest >= amount - 1 else 0
    holding, spare = [largest] + [least] * (amount - 1), total - largest - least * (amount - 1)
    while spare > 0:
        movable = [i for i in range(1, amount) if holding[i] < largest] or [i for i in range(1, amount) if holding[i] < bound]
        mass, remaining = sum([weights[i] for i in movable]), spare
        for i in movable:
            extra = min(bound - holding[i], max(1, remaining * weights[i] // mass), spare)
            holding[i] = holding[i] + extra
            spare = spare - extra
    return np.array(holding)


def centred(rng, extent, scale, bound, cuts=(), held_as=jnp.bfloat16):
    drawn = scale * jax.random.normal(rng, extent, jnp.float32)
    if cuts:
        drawn = drawn * shard_levels(rng, extent, cuts, -0.22, 0.18)
    return jnp.clip(drawn, -bound, bound).astype(held_as)


def setup_inputs(seed: int = 0, part: int = 0) -> dict:
    streams_of = jax.random.split(jax.random.key(seed), 12)
    part_keys = jax.random.split(jax.random.fold_in(streams_of[11], part), 12)
    tokens = centred(part_keys[0], (REQS, D), 1.0, 6.0, ((0, 16),))
    queries = draw_queries(jax.random.fold_in(jax.random.fold_in(streams_of[11], part), 71), part)
    fresh_kv = draw_fresh_kv(jax.random.fold_in(jax.random.fold_in(streams_of[11], part), 71), part)
    old_cache = draw_old_cache(jax.random.fold_in(jax.random.fold_in(streams_of[11], part), 71), part)
    old_slot = draw_old_slot(jax.random.fold_in(jax.random.fold_in(streams_of[11], part), 71), part)
    new_owner_keys = jax.random.split(jax.random.fold_in(part_keys[5], 1), REQS // REQ_DEV)
    new_owner_turns = jax.random.permutation(jax.random.fold_in(part_keys[5], 3), REQS // REQ_DEV)
    new_owner = jax.vmap(lambda own, number: shared_out(jax.random.fold_in(part_keys[5], 2), own, number, REQ_DEV, N_GRP, 1, PER_PEER, 2))(new_owner_keys, new_owner_turns).reshape((REQS, 1))
    lengths = draw_lengths(jax.random.fold_in(jax.random.fold_in(streams_of[11], part), 71), part)
    norm_gain = jnp.clip(1.0 + 0.18 * jax.random.normal(part_keys[7], (D,), jnp.float32), 0.099609375, 1.8984375).astype(jnp.bfloat16)
    gate_weight = centred(part_keys[8], (D, FF), D ** -0.5, 0.09375, ((1, 16),))
    up_weight = centred(part_keys[9], (D, FF), D ** -0.5, 0.09375, ((1, 16),))
    down_weight = centred(part_keys[10], (FF, D), FF ** -0.5, 0.046875, ((0, 16),))
    return {"tokens": tokens, "queries": queries, "fresh_kv": fresh_kv, "old_cache": old_cache, "old_slot": old_slot, "new_owner": new_owner, "lengths": lengths, "norm_gain": norm_gain, "gate_weight": gate_weight, "up_weight": up_weight, "down_weight": down_weight}


def attend(cache_items, query_items, length_items):
    items = cache_items.shape[0]
    width = KVH * HD
    key_rows = cache_items[:, :, :width].reshape(items, CACHE, KVH, HD).astype(jnp.float32)
    value_rows = cache_items[:, :, width:].reshape(items, CACHE, KVH, HD).astype(jnp.float32)
    query_heads = query_items.reshape(items, KVH, QH // KVH, HD).astype(jnp.float32)
    scores = jnp.einsum('npkd,nkgd->nkgp', key_rows, query_heads) / jnp.sqrt(jnp.float32(HD))
    valid_mask = jnp.arange(CACHE)[None, :] <= length_items[:, None]
    scores = jnp.where(valid_mask[:, None, None, :], scores, -jnp.inf)
    row_max = lax.optimization_barrier(jnp.max(scores, axis=-1, keepdims=True))
    expd = jnp.exp(scores - row_max)
    row_total = lax.optimization_barrier(jnp.sum(expd, axis=-1, keepdims=True))
    weights = (expd / row_total).astype(jnp.bfloat16)
    result = jnp.einsum('nkgp,npkd->nkgd', weights.astype(jnp.float32), value_rows)
    return result.reshape(items, QH * HD).astype(jnp.bfloat16)

def reference(tokens, queries, fresh_kv, old_cache, old_slot, new_owner, lengths, norm_gain, gate_weight, up_weight, down_weight):
    requests = jnp.arange(REQS, dtype=jnp.int32)
    block_start = requests // REQ_DEV * REQ_DEV
    held_rows = old_cache[(block_start + old_slot).astype(jnp.int32)]
    positions = jnp.arange(CACHE, dtype=jnp.int32)
    updated = jnp.where(positions[None, :, None] == lengths[:, None, None], fresh_kv[:, None, :], held_rows)
    attended = attend(updated, queries, lengths)
    residual = tokens.astype(jnp.float32) + attended.astype(jnp.float32)
    meansq = lax.optimization_barrier(jnp.mean(residual * residual, axis=-1, keepdims=True))
    normed = (residual * lax.rsqrt(meansq + 1e-05) * norm_gain.astype(jnp.float32)).astype(jnp.bfloat16)
    gate_pre = jnp.dot(normed, gate_weight, preferred_element_type=jnp.float32)
    up_pre = jnp.dot(normed, up_weight, preferred_element_type=jnp.float32)
    hidden = (jax.nn.silu(gate_pre) * up_pre).astype(jnp.bfloat16)
    share = FF // N_GRP
    hidden_blocks = hidden.reshape(REQS, N_GRP, share).transpose(1, 0, 2)
    down_blocks = down_weight.reshape(N_GRP, share, D)

    def add_block(total, pieces):
        part_sum = jnp.dot(pieces[0], pieces[1], preferred_element_type=jnp.float32).astype(jnp.bfloat16)
        part_sum = lax.optimization_barrier(part_sum)
        return (total + part_sum.astype(jnp.float32), None)
    ffn_sum, unused = lax.scan(add_block, jnp.zeros((REQS, D), jnp.float32), (hidden_blocks, down_blocks))
    layer_out = (residual + ffn_sum).astype(jnp.bfloat16)
    target = new_owner[:, 0].reshape(N_GRP, REQ_DEV)
    onehot = (target[:, :, None] == jnp.arange(N_GRP, dtype=jnp.int32)[None, None, :]).astype(jnp.int32)
    rank_in = lax.optimization_barrier(jnp.sum((jnp.cumsum(onehot, axis=1) - onehot) * onehot, axis=-1)).reshape(REQS)
    new_slot = new_owner[:, 0] * SLOTS + requests // REQ_DEV * PER_PEER + rank_in
    new_cache = jnp.zeros((N_GRP * SLOTS, CACHE, 2 * KVH * HD), jnp.bfloat16).at[new_slot.astype(jnp.int32)].set(updated)
    return (layer_out, new_cache)
```

```python
import jax
import jax.numpy as jnp
from jax import lax
from jax.experimental import pallas as pl
from jax.experimental.pallas import tpu as pltpu
from jax.sharding import PartitionSpec as P

KVH = 4
HD = 128
PER_PEER = 4
SIDE = 4
HALF = 16
MESH = pl.DeviceIdType.MESH
ANY = pl.BlockSpec(memory_space=pl.ANY)
SMEM = pl.BlockSpec(memory_space=pltpu.SMEM)
VMEM = pl.BlockSpec(memory_space=pltpu.VMEM)
PEERS = (
    (2, 2), (1, 0), (0, 1), (3, 0), (0, 3), (2, 1), (1, 2), (2, 3),
    (3, 2), (2, 0), (0, 2), (1, 1), (3, 3), (1, 3), (3, 1),
)


def pack_kernel(slot_ref, owner_ref, len_ref, fresh_ref, cache_ref, upd_ref, send_ref,
                held, zero, count, place, in_sem, upd_sem, send_sem):
    rows, cache_len = held.shape[0], held.shape[1]
    members = send_ref.shape[0] // PER_PEER
    for r in range(rows):
        pltpu.make_async_copy(cache_ref.at[slot_ref[r]], held.at[r], in_sem.at[r]).start()
    zero[...] = jnp.zeros_like(zero)
    for m in range(members):
        count[m] = 0
    for r in range(rows):
        owner = owner_ref[r, 0]
        rank = count[owner]
        place[r] = owner * PER_PEER + rank
        count[owner] = rank + 1
    for m in range(members):
        for k in range(PER_PEER):
            s = m * PER_PEER + k

            @pl.when(count[m] <= k)
            def _():
                pltpu.make_async_copy(zero, send_ref.at[s], send_sem.at[s]).start()

    position = lax.broadcasted_iota(jnp.int32, (cache_len, held.shape[2]), 0)
    for r in range(rows):
        pltpu.make_async_copy(cache_ref.at[0], held.at[r], in_sem.at[r]).wait()
        new = jnp.broadcast_to(fresh_ref[r : r + 1, :].astype(jnp.float32), position.shape)
        old = held[r].astype(jnp.float32)
        held[r] = jnp.where(position == len_ref[r], new, old).astype(held.dtype)
        s = place[r]
        pltpu.make_async_copy(held.at[r], send_ref.at[s], send_sem.at[s]).start()
        pltpu.make_async_copy(held.at[r], upd_ref.at[r], upd_sem.at[r]).start()
    for r in range(rows):
        pltpu.make_async_copy(held.at[r], upd_ref.at[r], upd_sem.at[r]).wait()
    for s in range(members * PER_PEER):
        pltpu.make_async_copy(zero, send_ref.at[s], send_sem.at[s]).wait()


def pack(old_slot, new_owner, lengths, fresh_kv, old_cache, members):
    rows, cache_len, width = old_cache.shape
    slots = members * PER_PEER
    return pl.pallas_call(
        pack_kernel,
        name="pack",
        out_shape=[
            jax.ShapeDtypeStruct((rows, cache_len, width), jnp.bfloat16),
            jax.ShapeDtypeStruct((slots, cache_len, width), jnp.bfloat16),
        ],
        in_specs=[SMEM, SMEM, SMEM, VMEM, ANY],
        out_specs=[ANY, ANY],
        scratch_shapes=[
            pltpu.VMEM((rows, cache_len, width), jnp.bfloat16),
            pltpu.VMEM((cache_len, width), jnp.bfloat16),
            pltpu.SMEM((members,), jnp.int32),
            pltpu.SMEM((rows,), jnp.int32),
            pltpu.SemaphoreType.DMA((rows,)),
            pltpu.SemaphoreType.DMA((rows,)),
            pltpu.SemaphoreType.DMA((slots,)),
        ],
        compiler_params=pltpu.CompilerParams(vmem_limit_bytes=16 << 20),
    )(old_slot, new_owner, lengths, fresh_kv, old_cache)


def layer_kernel(len_ref, tok_hbm, q_hbm, gain_hbm, upd_hbm, send_hbm, gate_hbm, up_hbm, down_hbm,
                 newc_ref, out_ref,
                 tok, query, gain, upd, w_in, w_down, full, parts, hidden, residual,
                 r1in, r1own, r1fwd, r2in, r2own, r2fwd,
                 load_sem, w_sem, mig_send, mig_recv, mig_local,
                 ag_send, ag_recv, rs_send, rs_recv):
    rows, width = tok.shape
    mid = width // 2
    left, right = pl.ds(0, mid), pl.ds(mid, mid)
    grp, rep = lax.axis_index("grp"), lax.axis_index("rep")
    x, y = grp // SIDE, grp % SIDE

    def device(px, py):
        return ((px + SIDE) % SIDE * SIDE + (py + SIDE) % SIDE, rep)

    loads = [
        pltpu.make_async_copy(src, dst, load_sem.at[i])
        for i, (src, dst) in enumerate(((upd_hbm, upd), (q_hbm, query), (tok_hbm, tok), (gain_hbm, gain)))
    ]
    for c in loads:
        c.start()
    barrier = pltpu.get_barrier_semaphore()
    for dx, dy in PEERS:
        pl.semaphore_signal(barrier, inc=1, device_id=device(x + dx, y + dy), device_id_type=MESH)
    pl.semaphore_wait(barrier, len(PEERS))

    def migrate(i, k):
        dx, dy = PEERS[i]
        target = device(x + dx, y + dy)
        return pltpu.make_async_remote_copy(
            src_ref=send_hbm.at[target[0] * PER_PEER + k],
            dst_ref=newc_ref.at[grp * PER_PEER + k],
            send_sem=mig_send.at[i, k],
            recv_sem=mig_recv.at[i, k],
            device_id=target,
            device_id_type=MESH,
        )

    def migrate_round(k):
        for i in range(len(PEERS)):
            migrate(i, k).start()

    own_slots = pl.ds(grp * PER_PEER, PER_PEER)
    stay = pltpu.make_async_copy(send_hbm.at[own_slots], newc_ref.at[own_slots], mig_local)
    migrate_round(0)
    stay.start()

    tiles = w_in.shape[0]
    w_copies = []
    for j in range(tiles):
        cols = pl.ds(j * HD, HD)
        w_copies.append(pltpu.make_async_copy(gate_hbm.at[:, cols], w_in.at[j, :, pl.ds(0, HD)], w_sem.at[2 * j]))
        w_copies.append(pltpu.make_async_copy(up_hbm.at[:, cols], w_in.at[j, :, pl.ds(HD, HD)], w_sem.at[2 * j + 1]))
    w_copies.append(pltpu.make_async_copy(down_hbm, w_down, w_sem.at[2 * tiles]))
    for c in loads:
        c.wait()
    for c in w_copies:
        c.start()

    cache_len = upd.shape[1]
    cols_n = rows * cache_len
    row_of = lax.broadcasted_iota(jnp.int32, (rows, cols_n), 0)
    col_of = lax.broadcasted_iota(jnp.int32, (rows, cols_n), 1)
    length = jnp.zeros((8, cols_n), jnp.int32)
    request = lax.broadcasted_iota(jnp.int32, (8, cols_n), 1) // cache_len
    for r in range(rows):
        length = jnp.where(request == r, len_ref[r], length)
    length = jnp.concatenate([length] * (rows // 8), axis=0)
    valid = (col_of // cache_len == row_of) & (col_of % cache_len <= length)
    bias = jnp.where(valid, 0.0, -1e30).astype(jnp.float32)
    heads_per = width // HD // KVH
    bias = jnp.concatenate([bias] * heads_per, axis=0)
    for g in range(KVH):
        keys = upd[:, :, g * HD : (g + 1) * HD].reshape(cols_n, HD)
        values = upd[:, :, (KVH + g) * HD : (KVH + g + 1) * HD].reshape(cols_n, HD)
        heads = [query[:, (g * heads_per + h) * HD : (g * heads_per + h + 1) * HD] for h in range(heads_per)]
        scores = lax.dot_general(
            jnp.concatenate(heads, axis=0), keys, (((1,), (1,)), ((), ())), preferred_element_type=jnp.float32
        )
        scores = scores * (HD**-0.5) + bias
        expd = jnp.exp(scores - jnp.max(scores, axis=1, keepdims=True))
        weights = (expd * (1.0 / jnp.sum(expd, axis=1, keepdims=True))).astype(jnp.bfloat16)
        attended = jnp.dot(weights, values, preferred_element_type=jnp.float32).astype(jnp.bfloat16)
        for h in range(heads_per):
            at = slice((g * heads_per + h) * HD, (g * heads_per + h + 1) * HD)
            residual[:, at] = attended[h * rows : (h + 1) * rows].astype(jnp.float32) + tok[:, at].astype(jnp.float32)
    res = residual[...]
    meansq = jnp.mean(res * res, axis=1, keepdims=True)
    normed = (res * lax.rsqrt(meansq + 1e-05) * gain[...].astype(jnp.float32)).astype(jnp.bfloat16)
    full[x, y] = normed.reshape(2, HALF, width)

    def peer(h, da, db):
        return device(x + da, y + db) if h == 0 else device(x + db, y + da)

    def block(h, da, db):
        px, py = (da, db) if h == 0 else (db, da)
        return ((x + px + SIDE) % SIDE, (y + py + SIDE) % SIDE, h)

    def gather_copy(n, h, da, db, cols, ta, tb):
        ref = full.at[(*block(h, da, db), slice(None), cols)]
        return pltpu.make_async_remote_copy(
            src_ref=ref, dst_ref=ref, send_sem=ag_send.at[h, n], recv_sem=ag_recv.at[h, n],
            device_id=peer(h, ta, tb), device_id_type=MESH,
        )

    everything = pl.ds(0, width)
    sent = []

    def go(copy):
        copy.start()
        sent.append(copy)
        return copy

    ORIGINS = (0, -1, 1, 2)

    def first(h, s):
        return gather_copy(0 if s > 0 else 1, h, 0, 0, everything, s, 0)

    def first_forward(h, s):
        return gather_copy(2 if s > 0 else 3, h, -s, 0, left if s > 0 else right, s, 0)

    def second(h, i, s):
        return gather_copy(4 + 2 * i + (s < 0), h, ORIGINS[i], 0, everything, 0, s)

    def second_forward(h, i, s):
        return gather_copy(12 + 2 * i + (s < 0), h, ORIGINS[i], -s, left if s > 0 else right, 0, s)

    both = (1, -1)
    for h in range(2):
        for s in both:
            go(first(h, s))
    for h in range(2):
        for s in both:
            go(second(h, 0, s))
    for i, s in ((1, 1), (2, -1)):
        for h in range(2):
            first(h, s).wait_recv()
            go(first_forward(h, s))
            for t in both:
                go(second(h, i, t))
    for h in range(2):
        for s in both:
            second(h, 0, s).wait_recv()
            go(second_forward(h, 0, s))
    for h in range(2):
        for s in both:
            first_forward(h, s).wait_recv()
        for t in both:
            go(second(h, 3, t))
    for i in (1, 2, 3):
        for h in range(2):
            for s in both:
                second(h, i, s).wait_recv()
                go(second_forward(h, i, s))
    for i in range(4):
        for h in range(2):
            for s in both:
                second_forward(h, i, s).wait_recv()

    migrate_round(1)
    for c in w_copies:
        c.wait()
    all_rows = SIDE * SIDE * rows

    def up_tile(j, carry):
        pre = jnp.dot(full[...].reshape(all_rows, width), w_in[j], preferred_element_type=jnp.float32)
        gate_pre, up_pre = pre[:, :HD], pre[:, HD:]
        act = gate_pre / (1.0 + jnp.exp(-gate_pre)) * up_pre
        hidden[:, pl.ds(pl.multiple_of(j * HD, HD), HD)] = act.astype(jnp.bfloat16)
        return carry

    lax.fori_loop(0, tiles, up_tile, 0)
    step = 2 * HD

    def down_tile(n, carry):
        cols = pl.ds(pl.multiple_of(n * step, step), step)
        part = jnp.dot(hidden[...], w_down[:, cols], preferred_element_type=jnp.float32)
        parts[:, :, :, :, cols] = part.astype(jnp.bfloat16).reshape(SIDE, SIDE, 2, HALF, step)
        return carry

    lax.fori_loop(0, width // step, down_tile, 0)

    def dest(h, stage, d):
        if stage == 0:
            b = ((y if h == 0 else x) + d + SIDE) % SIDE
            return (slice(None), b, h) if h == 0 else (b, slice(None), h)
        return block(h, d, 0)

    def scatter_copy(n, h, stage, d, cols, s, buf):
        return pltpu.make_async_remote_copy(
            src_ref=parts.at[(*dest(h, stage, d), slice(None), cols)],
            dst_ref=buf.at[h, 0 if s > 0 else 1],
            send_sem=rs_send.at[h, stage, n], recv_sem=rs_recv.at[h, stage, n],
            device_id=peer(h, 0, s) if stage == 0 else peer(h, s, 0), device_id_type=MESH,
        )

    bufs = ((r1in, r1own, r1fwd), (r2in, r2own, r2fwd))

    def far(h, stage, s):
        return scatter_copy(0 if s > 0 else 1, h, stage, 2, left if s > 0 else right, s, bufs[stage][0])

    def near(h, stage, s):
        return scatter_copy(2 if s > 0 else 3, h, stage, s, right if s > 0 else left, s, bufs[stage][1])

    def forward(h, stage, s):
        return scatter_copy(4 if s > 0 else 5, h, stage, s, left if s > 0 else right, s, bufs[stage][2])

    def f32(v):
        return v.astype(jnp.float32)

    for h in range(2):
        for s in both:
            go(far(h, 0, s))
    for h in range(2):
        for s in both:
            go(near(h, 0, s))
    migrate_round(2)
    migrate_round(3)
    for stage in range(2):
        got_far, got_near, got_forward = bufs[stage]
        for h in range(2):
            for s in both:
                far(h, stage, s).wait_recv()
                at = (*dest(h, stage, s), slice(None), left if s > 0 else right)
                parts[at] = (f32(parts[at]) + f32(got_far[h, 0 if s > 0 else 1])).astype(jnp.bfloat16)
                go(forward(h, stage, s))
        for h in range(2):
            sums = []
            for s in both:
                near(h, stage, s).wait_recv()
            for s in both:
                forward(h, stage, s).wait_recv()
                cols = left if s > 0 else right
                at = (*dest(h, stage, 0), slice(None), cols)
                way = 0 if s > 0 else 1
                total = f32(parts[at]) + f32(got_near[h, 1 - way]) + f32(got_forward[h, way])
                if stage == 0:
                    parts[at] = total.astype(jnp.bfloat16)
                else:
                    mine = pl.ds(h * HALF, HALF)
                    tok[mine, cols] = (residual[mine, cols] + total).astype(jnp.bfloat16)
            if stage == 0:
                for s in both:
                    go(far(h, 1, s))
                for s in both:
                    go(near(h, 1, s))
    result = pltpu.make_async_copy(tok, out_ref, load_sem.at[0])
    result.start()

    for copy in sent:
        copy.wait_send()
    stay.wait()
    for k in range(PER_PEER):
        for i in range(len(PEERS)):
            migrate(i, k).wait()
    result.wait()


def layer(lengths, tokens, queries, gain, upd, send, gate_weight, up_weight, down_weight):
    rows, width = tokens.shape
    share = gate_weight.shape[1]
    slots, cache_len, kv_width = send.shape
    mid = width // 2
    bf16 = jnp.bfloat16
    return pl.pallas_call(
        layer_kernel,
        name="layer",
        out_shape=[
            jax.ShapeDtypeStruct((slots, cache_len, kv_width), bf16),
            jax.ShapeDtypeStruct((rows, width), bf16),
        ],
        in_specs=[SMEM] + [ANY] * 8,
        out_specs=[ANY, ANY],
        scratch_shapes=[
            pltpu.VMEM((rows, width), bf16),
            pltpu.VMEM((rows, width), bf16),
            pltpu.VMEM((1, width), bf16),
            pltpu.VMEM(upd.shape, bf16),
            pltpu.VMEM((share // HD, width, 2 * HD), bf16),
            pltpu.VMEM((share, width), bf16),
            pltpu.VMEM((SIDE, SIDE, 2, HALF, width), bf16),
            pltpu.VMEM((SIDE, SIDE, 2, HALF, width), bf16),
            pltpu.VMEM((SIDE * SIDE * rows, share), bf16),
            pltpu.VMEM((rows, width), jnp.float32),
            pltpu.VMEM((2, 2, SIDE, HALF, mid), bf16),
            pltpu.VMEM((2, 2, SIDE, HALF, mid), bf16),
            pltpu.VMEM((2, 2, SIDE, HALF, mid), bf16),
            pltpu.VMEM((2, 2, HALF, mid), bf16),
            pltpu.VMEM((2, 2, HALF, mid), bf16),
            pltpu.VMEM((2, 2, HALF, mid), bf16),
            pltpu.SemaphoreType.DMA((4,)),
            pltpu.SemaphoreType.DMA((2 * (share // HD) + 1,)),
            pltpu.SemaphoreType.DMA((len(PEERS), PER_PEER)),
            pltpu.SemaphoreType.DMA((len(PEERS), PER_PEER)),
            pltpu.SemaphoreType.DMA,
            pltpu.SemaphoreType.DMA((2, 20)),
            pltpu.SemaphoreType.DMA((2, 20)),
            pltpu.SemaphoreType.DMA((2, 2, 6)),
            pltpu.SemaphoreType.DMA((2, 2, 6)),
        ],
        compiler_params=pltpu.CompilerParams(
            collective_id=0, has_side_effects=True, vmem_limit_bytes=60 << 20
        ),
    )(lengths, tokens, queries, gain, upd, send, gate_weight, up_weight, down_weight)


def finish_kernel(newc_ref, out_ref, newc_out, out_out, sems):
    pieces = sems.shape[0] - 1
    size = newc_ref.shape[0] // pieces
    copies = [
        pltpu.make_async_copy(newc_ref.at[pl.ds(i * size, size)], newc_out.at[pl.ds(i * size, size)], sems.at[i])
        for i in range(pieces)
    ]
    copies.append(pltpu.make_async_copy(out_ref, out_out, sems.at[pieces]))
    for c in copies:
        c.start()
    for c in copies:
        c.wait()


def finish(newc, out):
    return pl.pallas_call(
        finish_kernel,
        name="finish",
        out_shape=[jax.ShapeDtypeStruct(newc.shape, newc.dtype), jax.ShapeDtypeStruct(out.shape, out.dtype)],
        in_specs=[ANY, ANY],
        out_specs=[ANY, ANY],
        scratch_shapes=[pltpu.SemaphoreType.DMA((17,))],
    )(newc, out)


def per_device(
    tokens,
    queries,
    fresh_kv,
    old_cache,
    old_slot,
    new_owner,
    lengths,
    norm_gain,
    gate_weight,
    up_weight,
    down_weight,
):
    members = lax.axis_size("grp")
    upd, send = pack(old_slot, new_owner, lengths, fresh_kv, old_cache, members)
    newc, out = layer(
        lengths, tokens, queries, norm_gain.reshape(1, -1), upd, send, gate_weight, up_weight, down_weight
    )
    new_cache, layer_out = finish(newc, out)
    return (layer_out, new_cache)


def solution(mesh):
    placed = (
        P(("rep", "grp"), None),
        P(("rep", "grp"), None),
        P(("rep", "grp"), None),
        P(("rep", "grp"), None, None),
        P(("rep", "grp")),
        P(("rep", "grp"), None),
        P(("rep", "grp")),
        P("rep"),
        P("rep", "grp"),
        P("rep", "grp"),
        P(("rep", "grp"), None),
    )
    return jax.shard_map(
        per_device,
        mesh=mesh,
        in_specs=placed,
        out_specs=(P(("rep", "grp"), None), P(("rep", "grp"), None, None)),
        check_vma=False,
    )
```

```python
import jax
import jax.numpy as jnp
from jax import lax
from jax.experimental import pallas as pl
from jax.experimental.pallas import tpu as pltpu
from jax.sharding import PartitionSpec as P

KVH = 4
HD = 128
PER_PEER = 4
SIDE = 4
HALF = 16
MESH = pl.DeviceIdType.MESH
ANY = pl.BlockSpec(memory_space=pl.ANY)
PEERS = (
    (2, 2), (1, 0), (0, 1), (3, 0), (0, 3), (2, 1), (1, 2), (2, 3),
    (3, 2), (2, 0), (0, 2), (1, 1), (3, 3), (1, 3), (3, 1),
)


def layer_kernel(tok_hbm, q_hbm, fresh_hbm, cache_hbm, slot_hbm, owner_hbm, len_hbm, gain_hbm,
                 gate_hbm, up_hbm, down_hbm,
                 newc_ref, out_ref,
                 slot_at, owner_at, len_at, table, table_at,
                 tok, query, fresh, cache, gain, upd, send, w_in, w_down, full, parts, hidden, residual,
                 r1in, r1own, r1fwd, r2in, r2own, r2fwd,
                 load_sem, w_sem, mig_send, mig_recv, mig_local,
                 ag_send, ag_recv, rs_send, rs_recv):
    rows, width = tok.shape
    mid = width // 2
    left, right = pl.ds(0, mid), pl.ds(mid, mid)
    grp, rep = lax.axis_index("grp"), lax.axis_index("rep")
    x, y = grp // SIDE, grp % SIDE

    def device(px, py):
        return ((px + SIDE) % SIDE * SIDE + (py + SIDE) % SIDE, rep)

    pairs = (
        (slot_hbm, slot_at), (owner_hbm, owner_at), (len_hbm, len_at), (cache_hbm, cache), (fresh_hbm, fresh),
        (q_hbm, query), (tok_hbm, tok), (gain_hbm, gain),
    )
    loads = [pltpu.make_async_copy(src, dst, load_sem.at[i]) for i, (src, dst) in enumerate(pairs)]
    for c in loads:
        c.start()
    barrier = pltpu.get_barrier_semaphore()
    for dx, dy in PEERS:
        pl.semaphore_signal(barrier, inc=1, device_id=device(x + dx, y + dy), device_id_type=MESH)

    cache_len, kv_width = cache.shape[1], cache.shape[2]
    for c in loads[:3]:
        c.wait()
    lane = lax.broadcasted_iota(jnp.int32, (rows, 128), 1)
    sub = lax.broadcasted_iota(jnp.int32, (rows, 128), 0)
    owner_row = jnp.full((rows, 128), -1, jnp.int32)
    owner_col = jnp.zeros((rows, 128), jnp.int32)
    for r in range(rows):
        owner_row = jnp.where(lane == r, owner_at[r], owner_row)
        owner_col = jnp.where(sub == r, owner_at[r], owner_col)
    before = (owner_row == owner_col) & (lane < sub)
    rank = jnp.sum(before.astype(jnp.int32), axis=1, keepdims=True)
    fills = (owner_col * PER_PEER + rank == lane).astype(jnp.int32)
    table[...] = jnp.broadcast_to(rows + jnp.sum(fills * (sub - rows), axis=0, keepdims=True), table.shape)
    to_smem = pltpu.make_async_copy(table, table_at, load_sem.at[0])
    to_smem.start()

    for c in loads[3:5]:
        c.wait()
    position = lax.broadcasted_iota(jnp.int32, (cache_len, kv_width), 0)

    for r in range(rows):
        new = jnp.broadcast_to(fresh[r : r + 1, :].astype(jnp.float32), position.shape)
        old = cache[slot_at[r]].astype(jnp.float32)
        upd[r] = jnp.where(position == len_at[r], new, old).astype(upd.dtype)
    upd[rows] = jnp.zeros((cache_len, kv_width), upd.dtype)
    to_smem.wait()
    for k in range(PER_PEER):
        for m in range(SIDE * SIDE):
            send[m * PER_PEER + k] = upd[table_at[0, m * PER_PEER + k]]
    pl.semaphore_wait(barrier, len(PEERS))

    def migrate(i, k):
        dx, dy = PEERS[i]
        target = device(x + dx, y + dy)
        return pltpu.make_async_remote_copy(
            src_ref=send.at[target[0] * PER_PEER + k],
            dst_ref=newc_ref.at[grp * PER_PEER + k],
            send_sem=mig_send.at[i, k],
            recv_sem=mig_recv.at[i, k],
            device_id=target,
            device_id_type=MESH,
        )

    def migrate_round(k):
        for i in range(len(PEERS)):
            migrate(i, k).start()

    own_slots = pl.ds(grp * PER_PEER, PER_PEER)
    stay = pltpu.make_async_copy(send.at[own_slots], newc_ref.at[own_slots], mig_local)
    migrate_round(0)
    stay.start()

    tiles = w_in.shape[0]
    w_copies = []
    for j in range(tiles):
        cols = pl.ds(j * HD, HD)
        w_copies.append(pltpu.make_async_copy(gate_hbm.at[:, cols], w_in.at[j, :, pl.ds(0, HD)], w_sem.at[2 * j]))
        w_copies.append(pltpu.make_async_copy(up_hbm.at[:, cols], w_in.at[j, :, pl.ds(HD, HD)], w_sem.at[2 * j + 1]))
    w_copies.append(pltpu.make_async_copy(down_hbm, w_down, w_sem.at[2 * tiles]))
    for c in w_copies:
        c.start()
    for c in loads[5:]:
        c.wait()

    cols_n = rows * cache_len
    row_of = lax.broadcasted_iota(jnp.int32, (rows, cols_n), 0)
    col_of = lax.broadcasted_iota(jnp.int32, (rows, cols_n), 1)
    length = jnp.zeros((8, cols_n), jnp.int32)
    request = lax.broadcasted_iota(jnp.int32, (8, cols_n), 1) // cache_len
    for r in range(rows):
        length = jnp.where(request == r, len_at[r], length)
    length = jnp.concatenate([length] * (rows // 8), axis=0)
    valid = (col_of // cache_len == row_of) & (col_of % cache_len <= length)
    bias = jnp.where(valid, 0.0, -1e30).astype(jnp.float32)
    heads_per = width // HD // KVH
    bias = jnp.concatenate([bias] * heads_per, axis=0)
    for g in range(KVH):
        keys = upd[:rows, :, g * HD : (g + 1) * HD].reshape(cols_n, HD)
        values = upd[:rows, :, (KVH + g) * HD : (KVH + g + 1) * HD].reshape(cols_n, HD)
        heads = [query[:, (g * heads_per + h) * HD : (g * heads_per + h + 1) * HD] for h in range(heads_per)]
        scores = lax.dot_general(
            jnp.concatenate(heads, axis=0), keys, (((1,), (1,)), ((), ())), preferred_element_type=jnp.float32
        )
        scores = scores * (HD**-0.5) + bias
        expd = jnp.exp(scores - jnp.max(scores, axis=1, keepdims=True))
        weights = (expd * (1.0 / jnp.sum(expd, axis=1, keepdims=True))).astype(jnp.bfloat16)
        attended = jnp.dot(weights, values, preferred_element_type=jnp.float32).astype(jnp.bfloat16)
        for h in range(heads_per):
            at = slice((g * heads_per + h) * HD, (g * heads_per + h + 1) * HD)
            residual[:, at] = attended[h * rows : (h + 1) * rows].astype(jnp.float32) + tok[:, at].astype(jnp.float32)
    res = residual[...]
    meansq = jnp.mean(res * res, axis=1, keepdims=True)
    normed = (res * lax.rsqrt(meansq + 1e-05) * gain[...].astype(jnp.float32).reshape(1, width)).astype(jnp.bfloat16)
    full[x, y] = normed.reshape(2, HALF, width)

    def peer(h, da, db):
        return device(x + da, y + db) if h == 0 else device(x + db, y + da)

    def block(h, da, db):
        px, py = (da, db) if h == 0 else (db, da)
        return ((x + px + SIDE) % SIDE, (y + py + SIDE) % SIDE, h)

    def gather_copy(n, h, da, db, cols, ta, tb):
        ref = full.at[(*block(h, da, db), slice(None), cols)]
        return pltpu.make_async_remote_copy(
            src_ref=ref, dst_ref=ref, send_sem=ag_send.at[h, n], recv_sem=ag_recv.at[h, n],
            device_id=peer(h, ta, tb), device_id_type=MESH,
        )

    everything = pl.ds(0, width)
    sent = []

    def go(copy):
        copy.start()
        sent.append(copy)
        return copy

    ORIGINS = (0, -1, 1, 2)

    def first(h, s):
        return gather_copy(0 if s > 0 else 1, h, 0, 0, everything, s, 0)

    def first_forward(h, s):
        return gather_copy(2 if s > 0 else 3, h, -s, 0, left if s > 0 else right, s, 0)

    def second(h, i, s):
        return gather_copy(4 + 2 * i + (s < 0), h, ORIGINS[i], 0, everything, 0, s)

    def second_forward(h, i, s):
        return gather_copy(12 + 2 * i + (s < 0), h, ORIGINS[i], -s, left if s > 0 else right, 0, s)

    both = (1, -1)
    for h in range(2):
        for s in both:
            go(first(h, s))
    for h in range(2):
        for s in both:
            go(second(h, 0, s))
    for i, s in ((1, 1), (2, -1)):
        for h in range(2):
            first(h, s).wait_recv()
            go(first_forward(h, s))
            for t in both:
                go(second(h, i, t))
    for h in range(2):
        for s in both:
            second(h, 0, s).wait_recv()
            go(second_forward(h, 0, s))
    for h in range(2):
        for s in both:
            first_forward(h, s).wait_recv()
        for t in both:
            go(second(h, 3, t))
    for i in (1, 2, 3):
        for h in range(2):
            for s in both:
                second(h, i, s).wait_recv()
                go(second_forward(h, i, s))
    for i in range(4):
        for h in range(2):
            for s in both:
                second_forward(h, i, s).wait_recv()

    migrate_round(1)
    for c in w_copies:
        c.wait()
    all_rows = SIDE * SIDE * rows

    def up_tile(j, carry):
        pre = jnp.dot(full[...].reshape(all_rows, width), w_in[j], preferred_element_type=jnp.float32)
        gate_pre, up_pre = pre[:, :HD], pre[:, HD:]
        act = gate_pre / (1.0 + jnp.exp(-gate_pre)) * up_pre
        hidden[:, pl.ds(pl.multiple_of(j * HD, HD), HD)] = act.astype(jnp.bfloat16)
        return carry

    lax.fori_loop(0, tiles, up_tile, 0)
    step = 2 * HD

    def down_tile(n, carry):
        cols = pl.ds(pl.multiple_of(n * step, step), step)
        part = jnp.dot(hidden[...], w_down[:, cols], preferred_element_type=jnp.float32)
        parts[:, :, :, :, cols] = part.astype(jnp.bfloat16).reshape(SIDE, SIDE, 2, HALF, step)
        return carry

    lax.fori_loop(0, width // step, down_tile, 0)

    def dest(h, stage, d):
        if stage == 0:
            b = ((y if h == 0 else x) + d + SIDE) % SIDE
            return (slice(None), b, h) if h == 0 else (b, slice(None), h)
        return block(h, d, 0)

    def scatter_copy(n, h, stage, d, cols, s, buf):
        return pltpu.make_async_remote_copy(
            src_ref=parts.at[(*dest(h, stage, d), slice(None), cols)],
            dst_ref=buf.at[h, 0 if s > 0 else 1],
            send_sem=rs_send.at[h, stage, n], recv_sem=rs_recv.at[h, stage, n],
            device_id=peer(h, 0, s) if stage == 0 else peer(h, s, 0), device_id_type=MESH,
        )

    bufs = ((r1in, r1own, r1fwd), (r2in, r2own, r2fwd))

    def far(h, stage, s):
        return scatter_copy(0 if s > 0 else 1, h, stage, 2, left if s > 0 else right, s, bufs[stage][0])

    def near(h, stage, s):
        return scatter_copy(2 if s > 0 else 3, h, stage, s, right if s > 0 else left, s, bufs[stage][1])

    def forward(h, stage, s):
        return scatter_copy(4 if s > 0 else 5, h, stage, s, left if s > 0 else right, s, bufs[stage][2])

    def f32(v):
        return v.astype(jnp.float32)

    for h in range(2):
        for s in both:
            go(far(h, 0, s))
    for h in range(2):
        for s in both:
            go(near(h, 0, s))
    migrate_round(2)
    migrate_round(3)
    for stage in range(2):
        got_far, got_near, got_forward = bufs[stage]
        for h in range(2):
            for s in both:
                far(h, stage, s).wait_recv()
                at = (*dest(h, stage, s), slice(None), left if s > 0 else right)
                parts[at] = (f32(parts[at]) + f32(got_far[h, 0 if s > 0 else 1])).astype(jnp.bfloat16)
                go(forward(h, stage, s))
        for h in range(2):
            sums = []
            for s in both:
                near(h, stage, s).wait_recv()
            for s in both:
                forward(h, stage, s).wait_recv()
                cols = left if s > 0 else right
                at = (*dest(h, stage, 0), slice(None), cols)
                way = 0 if s > 0 else 1
                total = f32(parts[at]) + f32(got_near[h, 1 - way]) + f32(got_forward[h, way])
                if stage == 0:
                    parts[at] = total.astype(jnp.bfloat16)
                else:
                    mine = pl.ds(h * HALF, HALF)
                    tok[mine, cols] = (residual[mine, cols] + total).astype(jnp.bfloat16)
            if stage == 0:
                for s in both:
                    go(far(h, 1, s))
                for s in both:
                    go(near(h, 1, s))
    result = pltpu.make_async_copy(tok, out_ref, load_sem.at[0])
    result.start()

    for copy in sent:
        copy.wait_send()
    stay.wait()
    for k in range(PER_PEER):
        for i in range(len(PEERS)):
            migrate(i, k).wait()
    result.wait()


def layer(tokens, queries, fresh_kv, old_cache, old_slot, new_owner, lengths, gain, gate_weight, up_weight, down_weight):
    rows, width = tokens.shape
    share = gate_weight.shape[1]
    _, cache_len, kv_width = old_cache.shape
    slots = SIDE * SIDE * PER_PEER
    mid = width // 2
    bf16 = jnp.bfloat16
    return pl.pallas_call(
        layer_kernel,
        name="layer",
        out_shape=[
            jax.ShapeDtypeStruct((slots, cache_len, kv_width), bf16),
            jax.ShapeDtypeStruct((rows, width), bf16),
        ],
        in_specs=[ANY] * 11,
        out_specs=[ANY, ANY],
        scratch_shapes=[
            pltpu.SMEM((rows,), jnp.int32),
            pltpu.SMEM((rows,), jnp.int32),
            pltpu.SMEM((rows,), jnp.int32),
            pltpu.VMEM((8, 128), jnp.int32),
            pltpu.SMEM((8, 128), jnp.int32),
            pltpu.VMEM((rows, width), bf16),
            pltpu.VMEM((rows, width), bf16),
            pltpu.VMEM(fresh_kv.shape, bf16),
            pltpu.VMEM(old_cache.shape, bf16),
            pltpu.VMEM((width,), bf16),
            pltpu.VMEM((rows + 1, cache_len, kv_width), bf16),
            pltpu.VMEM((slots, cache_len, kv_width), bf16),
            pltpu.VMEM((share // HD, width, 2 * HD), bf16),
            pltpu.VMEM((share, width), bf16),
            pltpu.VMEM((SIDE, SIDE, 2, HALF, width), bf16),
            pltpu.VMEM((SIDE, SIDE, 2, HALF, width), bf16),
            pltpu.VMEM((SIDE * SIDE * rows, share), bf16),
            pltpu.VMEM((rows, width), jnp.float32),
            pltpu.VMEM((2, 2, SIDE, HALF, mid), bf16),
            pltpu.VMEM((2, 2, SIDE, HALF, mid), bf16),
            pltpu.VMEM((2, 2, SIDE, HALF, mid), bf16),
            pltpu.VMEM((2, 2, HALF, mid), bf16),
            pltpu.VMEM((2, 2, HALF, mid), bf16),
            pltpu.VMEM((2, 2, HALF, mid), bf16),
            pltpu.SemaphoreType.DMA((8,)),
            pltpu.SemaphoreType.DMA((2 * (share // HD) + 1,)),
            pltpu.SemaphoreType.DMA((len(PEERS), PER_PEER)),
            pltpu.SemaphoreType.DMA((len(PEERS), PER_PEER)),
            pltpu.SemaphoreType.DMA,
            pltpu.SemaphoreType.DMA((2, 20)),
            pltpu.SemaphoreType.DMA((2, 20)),
            pltpu.SemaphoreType.DMA((2, 2, 6)),
            pltpu.SemaphoreType.DMA((2, 2, 6)),
        ],
        compiler_params=pltpu.CompilerParams(
            collective_id=0, has_side_effects=True, vmem_limit_bytes=60 << 20
        ),
    )(
        tokens, queries, fresh_kv, old_cache, old_slot, new_owner, lengths, gain, gate_weight, up_weight, down_weight
    )


def finish_kernel(newc_ref, out_ref, newc_out, out_out, newc, out, in_sem, out_sem):
    pieces = in_sem.shape[0] - 1
    size = newc.shape[0] // pieces
    ins, outs = [], []
    for i in range(pieces):
        at = pl.ds(i * size, size)
        ins.append(pltpu.make_async_copy(newc_ref.at[at], newc.at[at], in_sem.at[i]))
        outs.append(pltpu.make_async_copy(newc.at[at], newc_out.at[at], out_sem.at[i]))
    ins.append(pltpu.make_async_copy(out_ref, out, in_sem.at[pieces]))
    outs.append(pltpu.make_async_copy(out, out_out, out_sem.at[pieces]))
    for c in ins:
        c.start()
    for c, d in zip(ins, outs):
        c.wait()
        d.start()
    for d in outs:
        d.wait()


def finish(newc, out):
    pieces = 8
    return pl.pallas_call(
        finish_kernel,
        name="finish",
        out_shape=[jax.ShapeDtypeStruct(newc.shape, newc.dtype), jax.ShapeDtypeStruct(out.shape, out.dtype)],
        in_specs=[ANY, ANY],
        out_specs=[ANY, ANY],
        scratch_shapes=[
            pltpu.VMEM(newc.shape, newc.dtype),
            pltpu.VMEM(out.shape, out.dtype),
            pltpu.SemaphoreType.DMA((pieces + 1,)),
            pltpu.SemaphoreType.DMA((pieces + 1,)),
        ],
        compiler_params=pltpu.CompilerParams(vmem_limit_bytes=60 << 20),
    )(newc, out)


def per_device(
    tokens,
    queries,
    fresh_kv,
    old_cache,
    old_slot,
    new_owner,
    lengths,
    norm_gain,
    gate_weight,
    up_weight,
    down_weight,
):
    newc, out = layer(
        tokens, queries, fresh_kv, old_cache, old_slot, new_owner.reshape(-1), lengths, norm_gain,
        gate_weight, up_weight, down_weight,
    )
    new_cache, layer_out = finish(newc, out)
    return (layer_out, new_cache)


def solution(mesh):
    placed = (
        P(("rep", "grp"), None),
        P(("rep", "grp"), None),
        P(("rep", "grp"), None),
        P(("rep", "grp"), None, None),
        P(("rep", "grp")),
        P(("rep", "grp"), None),
        P(("rep", "grp")),
        P("rep"),
        P("rep", "grp"),
        P("rep", "grp"),
        P(("rep", "grp"), None),
    )
    return jax.shard_map(
        per_device,
        mesh=mesh,
        in_specs=placed,
        out_specs=(P(("rep", "grp"), None), P(("rep", "grp"), None, None)),
        check_vma=False,
    )
```

```python
import jax
import jax.numpy as jnp
from jax import lax
from jax.experimental import pallas as pl
from jax.experimental.pallas import tpu as pltpu
from jax.sharding import PartitionSpec as P

FEED = (20, 0, 0, 0, 0, 0, 0, 0, 20, 6, 6, 4, 4)
PIECES = 2
KVH = 4
HD = 128
PER_PEER = 4
SIDE = 4
HALF = 16
MESH = pl.DeviceIdType.MESH
ANY = pl.BlockSpec(memory_space=pl.ANY)
PEERS = (
    (2, 2), (1, 0), (0, 1), (3, 0), (0, 3), (2, 1), (1, 2), (2, 3),
    (3, 2), (2, 0), (0, 2), (1, 1), (3, 3), (1, 3), (3, 1),
)


def layer_kernel(tok_hbm, q_hbm, fresh_hbm, cache_hbm, slot_hbm, owner_hbm, len_hbm, gain_hbm,
                 gate_hbm, up_hbm, down_hbm,
                 newc_ref, out_ref,
                 slot_at, owner_at, len_at, table, table_at,
                 tok, query, fresh, cache, gain, upd, send, w_in, w_down, full, parts, hidden, residual,
                 r1in, r1own, r1fwd, r2in, r2own, r2fwd,
                 load_sem, w_sem, mig_send, mig_recv, mig_local,
                 ag_send, ag_recv, rs_send, rs_recv):
    rows, width = tok.shape
    mid = width // 2
    left, right = pl.ds(0, mid), pl.ds(mid, mid)
    grp, rep = lax.axis_index("grp"), lax.axis_index("rep")
    x, y = grp // SIDE, grp % SIDE

    def device(px, py):
        return ((px + SIDE) % SIDE * SIDE + (py + SIDE) % SIDE, rep)

    pairs = (
        (slot_hbm, slot_at), (owner_hbm, owner_at), (len_hbm, len_at), (cache_hbm, cache), (fresh_hbm, fresh),
        (q_hbm, query), (tok_hbm, tok), (gain_hbm, gain),
    )
    loads = [pltpu.make_async_copy(src, dst, load_sem.at[i]) for i, (src, dst) in enumerate(pairs)]
    for c in loads:
        c.start()
    barrier = pltpu.get_barrier_semaphore()
    for dx, dy in PEERS:
        pl.semaphore_signal(barrier, inc=1, device_id=device(x + dx, y + dy), device_id_type=MESH)

    cache_len, kv_width = cache.shape[1], cache.shape[2]
    for c in loads[:3]:
        c.wait()
    lane = lax.broadcasted_iota(jnp.int32, (rows, 128), 1)
    sub = lax.broadcasted_iota(jnp.int32, (rows, 128), 0)
    owner_row = jnp.full((rows, 128), -1, jnp.int32)
    owner_col = jnp.zeros((rows, 128), jnp.int32)
    for r in range(rows):
        owner_row = jnp.where(lane == r, owner_at[r], owner_row)
        owner_col = jnp.where(sub == r, owner_at[r], owner_col)
    before = (owner_row == owner_col) & (lane < sub)
    rank = jnp.sum(before.astype(jnp.int32), axis=1, keepdims=True)
    fills = (owner_col * PER_PEER + rank == lane).astype(jnp.int32)
    table[...] = jnp.broadcast_to(rows + jnp.sum(fills * (sub - rows), axis=0, keepdims=True), table.shape)
    to_smem = pltpu.make_async_copy(table, table_at, load_sem.at[0])
    to_smem.start()

    for c in loads[3:5]:
        c.wait()
    position = lax.broadcasted_iota(jnp.int32, (cache_len, kv_width), 0)

    for r in range(rows):
        new = jnp.broadcast_to(fresh[r : r + 1, :].astype(jnp.float32), position.shape)
        old = cache[slot_at[r]].astype(jnp.float32)
        upd[r] = jnp.where(position == len_at[r], new, old).astype(upd.dtype)
    upd[rows] = jnp.zeros((cache_len, kv_width), upd.dtype)
    to_smem.wait()
    for k in range(PER_PEER):
        for m in range(SIDE * SIDE):
            send[m * PER_PEER + k] = upd[table_at[0, m * PER_PEER + k]]
    pl.semaphore_wait(barrier, len(PEERS))

    def slots_copy(amount, send_sem, recv_sem):
        return pltpu.make_async_remote_copy(
            src_ref=send.at[pl.ds(0, amount)], dst_ref=newc_ref.at[pl.ds(0, amount)],
            send_sem=send_sem, recv_sem=recv_sem, device_id=device(x + 1, y), device_id_type=MESH,
        )

    def migrate(i, k, group):
        dx, dy = PEERS[i]
        target = device(x + dx, y + dy)
        return pltpu.make_async_remote_copy(
            src_ref=send.at[target[0] * PER_PEER + k],
            dst_ref=newc_ref.at[grp * PER_PEER + k],
            send_sem=mig_send.at[group],
            recv_sem=mig_recv.at[group],
            device_id=target,
            device_id_type=MESH,
        )

    queue = [(i, k) for k in range(PER_PEER) for i in range(len(PEERS))]

    def feed(point):
        for _ in range(FEED[point]):
            migrate(*queue.pop(0), point).start()

    own_slots = pl.ds(grp * PER_PEER, PER_PEER)
    stay = pltpu.make_async_copy(send.at[own_slots], newc_ref.at[own_slots], mig_local)
    feed(0)
    stay.start()

    tiles = w_in.shape[0]
    w_copies = []
    for j in range(tiles):
        cols = pl.ds(j * HD, HD)
        w_copies.append(pltpu.make_async_copy(gate_hbm.at[:, cols], w_in.at[j, :, pl.ds(0, HD)], w_sem.at[2 * j]))
        w_copies.append(pltpu.make_async_copy(up_hbm.at[:, cols], w_in.at[j, :, pl.ds(HD, HD)], w_sem.at[2 * j + 1]))
    w_copies.append(pltpu.make_async_copy(down_hbm, w_down, w_sem.at[2 * tiles]))
    for c in w_copies:
        c.start()
    for c in loads[5:]:
        c.wait()

    cols_n = rows * cache_len
    row_of = lax.broadcasted_iota(jnp.int32, (rows, cols_n), 0)
    col_of = lax.broadcasted_iota(jnp.int32, (rows, cols_n), 1)
    length = jnp.zeros((8, cols_n), jnp.int32)
    request = lax.broadcasted_iota(jnp.int32, (8, cols_n), 1) // cache_len
    for r in range(rows):
        length = jnp.where(request == r, len_at[r], length)
    length = jnp.concatenate([length] * (rows // 8), axis=0)
    valid = (col_of // cache_len == row_of) & (col_of % cache_len <= length)
    bias = jnp.where(valid, 0.0, -1e30).astype(jnp.float32)
    heads_per = width // HD // KVH
    bias = jnp.concatenate([bias] * heads_per, axis=0)
    for g in range(KVH):
        keys = upd[:rows, :, g * HD : (g + 1) * HD].reshape(cols_n, HD)
        values = upd[:rows, :, (KVH + g) * HD : (KVH + g + 1) * HD].reshape(cols_n, HD)
        heads = [query[:, (g * heads_per + h) * HD : (g * heads_per + h + 1) * HD] for h in range(heads_per)]
        scores = lax.dot_general(
            jnp.concatenate(heads, axis=0), keys, (((1,), (1,)), ((), ())), preferred_element_type=jnp.float32
        )
        scores = scores * (HD**-0.5) + bias
        expd = jnp.exp(scores - jnp.max(scores, axis=1, keepdims=True))
        weights = (expd * (1.0 / jnp.sum(expd, axis=1, keepdims=True))).astype(jnp.bfloat16)
        attended = jnp.dot(weights, values, preferred_element_type=jnp.float32).astype(jnp.bfloat16)
        for h in range(heads_per):
            at = slice((g * heads_per + h) * HD, (g * heads_per + h + 1) * HD)
            residual[:, at] = attended[h * rows : (h + 1) * rows].astype(jnp.float32) + tok[:, at].astype(jnp.float32)
    res = residual[...]
    meansq = jnp.mean(res * res, axis=1, keepdims=True)
    normed = (res * lax.rsqrt(meansq + 1e-05) * gain[...].astype(jnp.float32).reshape(1, width)).astype(jnp.bfloat16)
    full[x, y] = normed.reshape(2, HALF, width)

    def peer(h, da, db):
        return device(x + da, y + db) if h == 0 else device(x + db, y + da)

    def block(h, da, db):
        px, py = (da, db) if h == 0 else (db, da)
        return ((x + px + SIDE) % SIDE, (y + py + SIDE) % SIDE, h)

    def gather_copy(n, h, da, db, cols, ta, tb):
        ref = full.at[(*block(h, da, db), slice(None), cols)]
        return pltpu.make_async_remote_copy(
            src_ref=ref, dst_ref=ref, send_sem=ag_send, recv_sem=ag_recv.at[h, n],
            device_id=peer(h, ta, tb), device_id_type=MESH,
        )

    everything = pl.ds(0, width)
    def go(copy):
        copy.start()

    ORIGINS = (0, -1, 1, 2)

    def first(h, s):
        return gather_copy(0 if s > 0 else 1, h, 0, 0, everything, s, 0)

    def first_forward(h, s):
        return gather_copy(2 if s > 0 else 3, h, -s, 0, left if s > 0 else right, s, 0)

    def second(h, i, s):
        return gather_copy(4 + 2 * i + (s < 0), h, ORIGINS[i], 0, everything, 0, s)

    def second_forward(h, i, s):
        return gather_copy(12 + 2 * i + (s < 0), h, ORIGINS[i], -s, left if s > 0 else right, 0, s)

    both = (1, -1)
    for h in range(2):
        for s in both:
            go(first(h, s))
    for h in range(2):
        for s in both:
            go(second(h, 0, s))
    feed(1)
    for i, s in ((1, 1), (2, -1)):
        for h in range(2):
            first(h, s).wait_recv()
            go(first_forward(h, s))
            for t in both:
                go(second(h, i, t))
    feed(2)
    for h in range(2):
        for s in both:
            second(h, 0, s).wait_recv()
            go(second_forward(h, 0, s))
    feed(3)
    for h in range(2):
        for s in both:
            first_forward(h, s).wait_recv()
        for t in both:
            go(second(h, 3, t))
    for i in (1, 2, 3):
        feed(3 + i)
        for h in range(2):
            for s in both:
                second(h, i, s).wait_recv()
                go(second_forward(h, i, s))
    feed(7)
    for i in range(4):
        for h in range(2):
            for s in both:
                second_forward(h, i, s).wait_recv()

    feed(8)
    for c in w_copies:
        c.wait()
    all_rows = SIDE * SIDE * rows

    def up_tile(j, carry):
        pre = jnp.dot(full[...].reshape(all_rows, width), w_in[j], preferred_element_type=jnp.float32)
        gate_pre, up_pre = pre[:, :HD], pre[:, HD:]
        act = gate_pre / (1.0 + jnp.exp(-gate_pre)) * up_pre
        hidden[:, pl.ds(pl.multiple_of(j * HD, HD), HD)] = act.astype(jnp.bfloat16)
        return carry

    lax.fori_loop(0, tiles, up_tile, 0)
    step = 2 * HD
    piece_width = width // PIECES
    half_width = piece_width // 2

    def down_piece(p):
        def down_tile(n, carry):
            cols = pl.ds(pl.multiple_of(n * step, step), step)
            part = jnp.dot(hidden[...], w_down[:, cols], preferred_element_type=jnp.float32)
            parts[:, :, :, :, cols] = part.astype(jnp.bfloat16).reshape(SIDE, SIDE, 2, HALF, step)
            return carry

        lax.fori_loop(p * piece_width // step, (p + 1) * piece_width // step, down_tile, 0)

    def dest(h, stage, d):
        if stage == 0:
            b = ((y if h == 0 else x) + d + SIDE) % SIDE
            return (slice(None), b, h) if h == 0 else (b, slice(None), h)
        return block(h, d, 0)

    def columns(p, side):
        return pl.ds(p * piece_width + side * half_width, half_width)

    def scatter_copy(n, p, h, stage, d, side, s, buf):
        return pltpu.make_async_remote_copy(
            src_ref=parts.at[(*dest(h, stage, d), slice(None), columns(p, side))],
            dst_ref=buf.at[p, h, 0 if s > 0 else 1],
            send_sem=rs_send, recv_sem=rs_recv.at[p, h, stage, n],
            device_id=peer(h, 0, s) if stage == 0 else peer(h, s, 0), device_id_type=MESH,
        )

    bufs = ((r1in, r1own, r1fwd), (r2in, r2own, r2fwd))

    def far(p, h, stage, s):
        return scatter_copy(0 if s > 0 else 1, p, h, stage, 2, 0 if s > 0 else 1, s, bufs[stage][0])

    def near(p, h, stage, s):
        return scatter_copy(2 if s > 0 else 3, p, h, stage, s, 1 if s > 0 else 0, s, bufs[stage][1])

    def forward(p, h, stage, s):
        return scatter_copy(4 if s > 0 else 5, p, h, stage, s, 0 if s > 0 else 1, s, bufs[stage][2])

    def f32(v):
        return v.astype(jnp.float32)

    def send_first(p, h, stage):
        for s in both:
            go(far(p, h, stage, s))
        for s in both:
            go(near(p, h, stage, s))

    def send_second(p, h, stage):
        for s in both:
            far(p, h, stage, s).wait_recv()
            side = 0 if s > 0 else 1
            at = (*dest(h, stage, s), slice(None), columns(p, side))
            parts[at] = (f32(parts[at]) + f32(bufs[stage][0][p, h, side])).astype(jnp.bfloat16)
            go(forward(p, h, stage, s))

    def sum_own(p, h, stage):
        for s in both:
            near(p, h, stage, s).wait_recv()
        for side, s in enumerate(both):
            forward(p, h, stage, s).wait_recv()
            cols = columns(p, side)
            at = (*dest(h, stage, 0), slice(None), cols)
            total = f32(parts[at]) + f32(bufs[stage][1][p, h, 1 - side]) + f32(bufs[stage][2][p, h, side])
            if stage == 0:
                parts[at] = total.astype(jnp.bfloat16)
            else:
                mine = pl.ds(h * HALF, HALF)
                tok[mine, cols] = (residual[mine, cols] + total).astype(jnp.bfloat16)

    for p in range(PIECES):
        down_piece(p)
        for h in range(2):
            send_first(p, h, 0)
    feed(9)
    for p in range(PIECES):
        for h in range(2):
            send_second(p, h, 0)
    feed(10)
    for p in range(PIECES):
        for h in range(2):
            sum_own(p, h, 0)
            send_first(p, h, 1)
    feed(11)
    for p in range(PIECES):
        for h in range(2):
            send_second(p, h, 1)
    feed(12)
    for p in range(PIECES):
        for h in range(2):
            sum_own(p, h, 1)
    result = pltpu.make_async_copy(tok, out_ref, load_sem.at[0])
    result.start()

    stay.wait()
    for point, amount in enumerate(FEED):
        if amount:
            together = slots_copy(amount, mig_send.at[point], mig_recv.at[point])
            together.wait_send()
            together.wait_recv()
    slots_copy(len(PEERS) * PER_PEER, ag_send, mig_local).wait_send()
    slots_copy(len(PEERS) * PER_PEER, rs_send, mig_local).wait_send()
    result.wait()


def layer(tokens, queries, fresh_kv, old_cache, old_slot, new_owner, lengths, gain, gate_weight, up_weight, down_weight):
    rows, width = tokens.shape
    share = gate_weight.shape[1]
    _, cache_len, kv_width = old_cache.shape
    slots = SIDE * SIDE * PER_PEER
    mid = width // PIECES // 2
    bf16 = jnp.bfloat16
    return pl.pallas_call(
        layer_kernel,
        name="layer",
        out_shape=[
            jax.ShapeDtypeStruct((slots, cache_len, kv_width), bf16),
            jax.ShapeDtypeStruct((rows, width), bf16),
        ],
        in_specs=[ANY] * 11,
        out_specs=[ANY, ANY],
        scratch_shapes=[
            pltpu.SMEM((rows,), jnp.int32),
            pltpu.SMEM((rows,), jnp.int32),
            pltpu.SMEM((rows,), jnp.int32),
            pltpu.VMEM((8, 128), jnp.int32),
            pltpu.SMEM((8, 128), jnp.int32),
            pltpu.VMEM((rows, width), bf16),
            pltpu.VMEM((rows, width), bf16),
            pltpu.VMEM(fresh_kv.shape, bf16),
            pltpu.VMEM(old_cache.shape, bf16),
            pltpu.VMEM((width,), bf16),
            pltpu.VMEM((rows + 1, cache_len, kv_width), bf16),
            pltpu.VMEM((slots, cache_len, kv_width), bf16),
            pltpu.VMEM((share // HD, width, 2 * HD), bf16),
            pltpu.VMEM((share, width), bf16),
            pltpu.VMEM((SIDE, SIDE, 2, HALF, width), bf16),
            pltpu.VMEM((SIDE, SIDE, 2, HALF, width), bf16),
            pltpu.VMEM((SIDE * SIDE * rows, share), bf16),
            pltpu.VMEM((rows, width), jnp.float32),
            pltpu.VMEM((PIECES, 2, 2, SIDE, HALF, mid), bf16),
            pltpu.VMEM((PIECES, 2, 2, SIDE, HALF, mid), bf16),
            pltpu.VMEM((PIECES, 2, 2, SIDE, HALF, mid), bf16),
            pltpu.VMEM((PIECES, 2, 2, HALF, mid), bf16),
            pltpu.VMEM((PIECES, 2, 2, HALF, mid), bf16),
            pltpu.VMEM((PIECES, 2, 2, HALF, mid), bf16),
            pltpu.SemaphoreType.DMA((8,)),
            pltpu.SemaphoreType.DMA((2 * (share // HD) + 1,)),
            pltpu.SemaphoreType.DMA((len(FEED),)),
            pltpu.SemaphoreType.DMA((len(FEED),)),
            pltpu.SemaphoreType.DMA,
            pltpu.SemaphoreType.DMA,
            pltpu.SemaphoreType.DMA((2, 20)),
            pltpu.SemaphoreType.DMA,
            pltpu.SemaphoreType.DMA((PIECES, 2, 2, 6)),
        ],
        compiler_params=pltpu.CompilerParams(
            collective_id=0, has_side_effects=True, vmem_limit_bytes=60 << 20
        ),
    )(
        tokens, queries, fresh_kv, old_cache, old_slot, new_owner, lengths, gain, gate_weight, up_weight, down_weight
    )


def finish_kernel(newc_ref, out_ref, newc_out, out_out, newc, out, in_sem, out_sem):
    pieces = in_sem.shape[0] - 1
    size = newc.shape[0] // pieces
    ins, outs = [], []
    for i in range(pieces):
        at = pl.ds(i * size, size)
        ins.append(pltpu.make_async_copy(newc_ref.at[at], newc.at[at], in_sem.at[i]))
        outs.append(pltpu.make_async_copy(newc.at[at], newc_out.at[at], out_sem.at[i]))
    ins.append(pltpu.make_async_copy(out_ref, out, in_sem.at[pieces]))
    outs.append(pltpu.make_async_copy(out, out_out, out_sem.at[pieces]))
    for c in ins:
        c.start()
    for c, d in zip(ins, outs):
        c.wait()
        d.start()
    for d in outs:
        d.wait()


def finish(newc, out):
    pieces = 8
    return pl.pallas_call(
        finish_kernel,
        name="finish",
        out_shape=[jax.ShapeDtypeStruct(newc.shape, newc.dtype), jax.ShapeDtypeStruct(out.shape, out.dtype)],
        in_specs=[ANY, ANY],
        out_specs=[ANY, ANY],
        scratch_shapes=[
            pltpu.VMEM(newc.shape, newc.dtype),
            pltpu.VMEM(out.shape, out.dtype),
            pltpu.SemaphoreType.DMA((pieces + 1,)),
            pltpu.SemaphoreType.DMA((pieces + 1,)),
        ],
        compiler_params=pltpu.CompilerParams(vmem_limit_bytes=60 << 20),
    )(newc, out)


def per_device(
    tokens,
    queries,
    fresh_kv,
    old_cache,
    old_slot,
    new_owner,
    lengths,
    norm_gain,
    gate_weight,
    up_weight,
    down_weight,
):
    newc, out = layer(
        tokens, queries, fresh_kv, old_cache, old_slot, new_owner.reshape(-1), lengths, norm_gain,
        gate_weight, up_weight, down_weight,
    )
    new_cache, layer_out = finish(newc, out)
    return (layer_out, new_cache)


def solution(mesh):
    placed = (
        P(("rep", "grp"), None),
        P(("rep", "grp"), None),
        P(("rep", "grp"), None),
        P(("rep", "grp"), None, None),
        P(("rep", "grp")),
        P(("rep", "grp"), None),
        P(("rep", "grp")),
        P("rep"),
        P("rep", "grp"),
        P("rep", "grp"),
        P(("rep", "grp"), None),
    )
    return jax.shard_map(
        per_device,
        mesh=mesh,
        in_specs=placed,
        out_specs=(P(("rep", "grp"), None), P(("rep", "grp"), None, None)),
        check_vma=False,
    )
```

```python
import jax
import jax.numpy as jnp
from jax import lax
from jax.experimental import pallas as pl
from jax.experimental.pallas import tpu as pltpu
from jax.sharding import PartitionSpec as P

FEED = (20, 0, 0, 0, 0, 0, 0, 3, 20, 6, 4, 4, 3)
PIECES = 2
KVH = 4
HD = 128
PER_PEER = 4
SIDE = 4
HALF = 16
MESH = pl.DeviceIdType.MESH
ANY = pl.BlockSpec(memory_space=pl.ANY)
PEERS = (
    (2, 2), (1, 0), (0, 1), (3, 0), (0, 3), (2, 1), (1, 2), (2, 3),
    (3, 2), (2, 0), (0, 2), (1, 1), (3, 3), (1, 3), (3, 1),
)


def layer_kernel(tok_hbm, q_hbm, fresh_hbm, cache_hbm, slot_hbm, owner_hbm, len_hbm, gain_hbm,
                 gate_hbm, up_hbm, down_hbm,
                 newc_ref, out_ref,
                 slot_at, owner_at, len_at, table, table_at,
                 tok, query, fresh, cache, gain, upd, send, w_in, w_down, full, parts, hidden, residual,
                 r1in, r1own, r1fwd, r2in, r2own, r2fwd,
                 load_sem, w_sem, mig_send, mig_recv, mig_local,
                 ag_send, ag_recv, rs_send, rs_recv):
    rows, width = tok.shape
    mid = width // 2
    left, right = pl.ds(0, mid), pl.ds(mid, mid)
    grp, rep = lax.axis_index("grp"), lax.axis_index("rep")
    x, y = grp // SIDE, grp % SIDE

    def device(px, py):
        return ((px + SIDE) % SIDE * SIDE + (py + SIDE) % SIDE, rep)

    pairs = (
        (slot_hbm, slot_at), (owner_hbm, owner_at), (len_hbm, len_at), (cache_hbm, cache), (fresh_hbm, fresh),
        (q_hbm, query), (tok_hbm, tok), (gain_hbm, gain),
    )
    loads = [pltpu.make_async_copy(src, dst, load_sem.at[i]) for i, (src, dst) in enumerate(pairs)]
    for c in loads:
        c.start()
    barrier = pltpu.get_barrier_semaphore()
    for dx, dy in PEERS:
        pl.semaphore_signal(barrier, inc=1, device_id=device(x + dx, y + dy), device_id_type=MESH)

    cache_len, kv_width = cache.shape[1], cache.shape[2]
    for c in loads[:3]:
        c.wait()
    lane = lax.broadcasted_iota(jnp.int32, (rows, 128), 1)
    sub = lax.broadcasted_iota(jnp.int32, (rows, 128), 0)
    owner_row = jnp.full((rows, 128), -1, jnp.int32)
    owner_col = jnp.zeros((rows, 128), jnp.int32)
    for r in range(rows):
        owner_row = jnp.where(lane == r, owner_at[r], owner_row)
        owner_col = jnp.where(sub == r, owner_at[r], owner_col)
    before = (owner_row == owner_col) & (lane < sub)
    rank = jnp.sum(before.astype(jnp.int32), axis=1, keepdims=True)
    fills = (owner_col * PER_PEER + rank == lane).astype(jnp.int32)
    table[...] = jnp.broadcast_to(rows + jnp.sum(fills * (sub - rows), axis=0, keepdims=True), table.shape)
    to_smem = pltpu.make_async_copy(table, table_at, load_sem.at[0])
    to_smem.start()

    for c in loads[3:5]:
        c.wait()
    position = lax.broadcasted_iota(jnp.int32, (cache_len, kv_width), 0)

    for r in range(rows):
        new = jnp.broadcast_to(fresh[r : r + 1, :].astype(jnp.float32), position.shape)
        old = cache[slot_at[r]].astype(jnp.float32)
        upd[r] = jnp.where(position == len_at[r], new, old).astype(upd.dtype)
    upd[rows] = jnp.zeros((cache_len, kv_width), upd.dtype)
    to_smem.wait()
    for k in range(PER_PEER):
        for m in range(SIDE * SIDE):
            send[m * PER_PEER + k] = upd[table_at[0, m * PER_PEER + k]]
    pl.semaphore_wait(barrier, len(PEERS))

    def slots_copy(amount, send_sem, recv_sem):
        return pltpu.make_async_remote_copy(
            src_ref=send.at[pl.ds(0, amount)], dst_ref=newc_ref.at[pl.ds(0, amount)],
            send_sem=send_sem, recv_sem=recv_sem, device_id=device(x + 1, y), device_id_type=MESH,
        )

    def migrate(i, k, group):
        dx, dy = PEERS[i]
        target = device(x + dx, y + dy)
        return pltpu.make_async_remote_copy(
            src_ref=send.at[target[0] * PER_PEER + k],
            dst_ref=newc_ref.at[grp * PER_PEER + k],
            send_sem=mig_send.at[group],
            recv_sem=mig_recv.at[group],
            device_id=target,
            device_id_type=MESH,
        )

    queue = [(i, k) for k in range(PER_PEER) for i in range(len(PEERS))]

    def feed(point):
        for _ in range(FEED[point]):
            migrate(*queue.pop(0), point).start()

    own_slots = pl.ds(grp * PER_PEER, PER_PEER)
    stay = pltpu.make_async_copy(send.at[own_slots], newc_ref.at[own_slots], mig_local)
    feed(0)
    stay.start()

    tiles = w_in.shape[0]
    w_copies = []
    for j in range(tiles):
        cols = pl.ds(j * HD, HD)
        w_copies.append(pltpu.make_async_copy(gate_hbm.at[:, cols], w_in.at[j, :, pl.ds(0, HD)], w_sem.at[2 * j]))
        w_copies.append(pltpu.make_async_copy(up_hbm.at[:, cols], w_in.at[j, :, pl.ds(HD, HD)], w_sem.at[2 * j + 1]))
    w_copies.append(pltpu.make_async_copy(down_hbm, w_down, w_sem.at[2 * tiles]))
    for c in w_copies:
        c.start()
    for c in loads[5:]:
        c.wait()

    cols_n = rows * cache_len
    row_of = lax.broadcasted_iota(jnp.int32, (rows, cols_n), 0)
    col_of = lax.broadcasted_iota(jnp.int32, (rows, cols_n), 1)
    length = jnp.zeros((8, cols_n), jnp.int32)
    request = lax.broadcasted_iota(jnp.int32, (8, cols_n), 1) // cache_len
    for r in range(rows):
        length = jnp.where(request == r, len_at[r], length)
    length = jnp.concatenate([length] * (rows // 8), axis=0)
    valid = (col_of // cache_len == row_of) & (col_of % cache_len <= length)
    bias = jnp.where(valid, 0.0, -1e30).astype(jnp.float32)
    heads_per = width // HD // KVH
    bias = jnp.concatenate([bias] * heads_per, axis=0)
    for g in range(KVH):
        keys = upd[:rows, :, g * HD : (g + 1) * HD].reshape(cols_n, HD)
        values = upd[:rows, :, (KVH + g) * HD : (KVH + g + 1) * HD].reshape(cols_n, HD)
        heads = [query[:, (g * heads_per + h) * HD : (g * heads_per + h + 1) * HD] for h in range(heads_per)]
        scores = lax.dot_general(
            jnp.concatenate(heads, axis=0), keys, (((1,), (1,)), ((), ())), preferred_element_type=jnp.float32
        )
        scores = scores * (HD**-0.5) + bias
        expd = jnp.exp(scores - jnp.max(scores, axis=1, keepdims=True))
        weights = (expd * (1.0 / jnp.sum(expd, axis=1, keepdims=True))).astype(jnp.bfloat16)
        attended = jnp.dot(weights, values, preferred_element_type=jnp.float32).astype(jnp.bfloat16)
        for h in range(heads_per):
            at = slice((g * heads_per + h) * HD, (g * heads_per + h + 1) * HD)
            residual[:, at] = attended[h * rows : (h + 1) * rows].astype(jnp.float32) + tok[:, at].astype(jnp.float32)
    res = residual[...]
    meansq = jnp.mean(res * res, axis=1, keepdims=True)
    normed = (res * lax.rsqrt(meansq + 1e-05) * gain[...].astype(jnp.float32).reshape(1, width)).astype(jnp.bfloat16)
    full[x, y] = normed.reshape(2, HALF, width)

    def peer(h, da, db):
        return device(x + da, y + db) if h == 0 else device(x + db, y + da)

    def block(h, da, db):
        px, py = (da, db) if h == 0 else (db, da)
        return ((x + px + SIDE) % SIDE, (y + py + SIDE) % SIDE, h)

    def gather_copy(n, h, da, db, cols, ta, tb):
        ref = full.at[(*block(h, da, db), slice(None), cols)]
        return pltpu.make_async_remote_copy(
            src_ref=ref, dst_ref=ref, send_sem=ag_send, recv_sem=ag_recv.at[h, n],
            device_id=peer(h, ta, tb), device_id_type=MESH,
        )

    everything = pl.ds(0, width)
    def go(copy):
        copy.start()

    ORIGINS = (0, -1, 1, 2)

    def first(h, s):
        return gather_copy(0 if s > 0 else 1, h, 0, 0, everything, s, 0)

    def first_forward(h, s):
        return gather_copy(2 if s > 0 else 3, h, -s, 0, left if s > 0 else right, s, 0)

    def second(h, i, s):
        return gather_copy(4 + 2 * i + (s < 0), h, ORIGINS[i], 0, everything, 0, s)

    def second_forward(h, i, s):
        return gather_copy(12 + 2 * i + (s < 0), h, ORIGINS[i], -s, left if s > 0 else right, 0, s)

    both = (1, -1)
    for h in range(2):
        for s in both:
            go(first(h, s))
    for h in range(2):
        for s in both:
            go(second(h, 0, s))
    feed(1)
    for i, s in ((1, 1), (2, -1)):
        for h in range(2):
            first(h, s).wait_recv()
            go(first_forward(h, s))
            for t in both:
                go(second(h, i, t))
    feed(2)
    for h in range(2):
        for s in both:
            second(h, 0, s).wait_recv()
            go(second_forward(h, 0, s))
    feed(3)
    for h in range(2):
        for s in both:
            first_forward(h, s).wait_recv()
        for t in both:
            go(second(h, 3, t))
    for i in (1, 2, 3):
        feed(3 + i)
        for h in range(2):
            for s in both:
                second(h, i, s).wait_recv()
                go(second_forward(h, i, s))
    feed(7)
    for i in range(4):
        for h in range(2):
            for s in both:
                second_forward(h, i, s).wait_recv()

    feed(8)
    for c in w_copies:
        c.wait()
    all_rows = SIDE * SIDE * rows

    def up_tile(j, carry):
        pre = jnp.dot(full[...].reshape(all_rows, width), w_in[j], preferred_element_type=jnp.float32)
        gate_pre, up_pre = pre[:, :HD], pre[:, HD:]
        act = gate_pre / (1.0 + jnp.exp(-gate_pre)) * up_pre
        hidden[:, pl.ds(pl.multiple_of(j * HD, HD), HD)] = act.astype(jnp.bfloat16)
        return carry

    lax.fori_loop(0, tiles, up_tile, 0)
    step = 2 * HD
    piece_width = width // PIECES
    half_width = piece_width // 2

    def down_piece(p):
        def down_tile(n, carry):
            cols = pl.ds(pl.multiple_of(n * step, step), step)
            part = jnp.dot(hidden[...], w_down[:, cols], preferred_element_type=jnp.float32)
            parts[:, :, :, :, cols] = part.astype(jnp.bfloat16).reshape(SIDE, SIDE, 2, HALF, step)
            return carry

        lax.fori_loop(p * piece_width // step, (p + 1) * piece_width // step, down_tile, 0)

    def dest(h, stage, d):
        if stage == 0:
            b = ((y if h == 0 else x) + d + SIDE) % SIDE
            return (slice(None), b, h) if h == 0 else (b, slice(None), h)
        return block(h, d, 0)

    def columns(p, side):
        return pl.ds(p * piece_width + side * half_width, half_width)

    def scatter_copy(n, p, h, stage, d, side, s, buf):
        return pltpu.make_async_remote_copy(
            src_ref=parts.at[(*dest(h, stage, d), slice(None), columns(p, side))],
            dst_ref=buf.at[p, h, 0 if s > 0 else 1],
            send_sem=rs_send, recv_sem=rs_recv.at[p, h, stage, n],
            device_id=peer(h, 0, s) if stage == 0 else peer(h, s, 0), device_id_type=MESH,
        )

    bufs = ((r1in, r1own, r1fwd), (r2in, r2own, r2fwd))

    def far(p, h, stage, s):
        return scatter_copy(0 if s > 0 else 1, p, h, stage, 2, 0 if s > 0 else 1, s, bufs[stage][0])

    def near(p, h, stage, s):
        return scatter_copy(2 if s > 0 else 3, p, h, stage, s, 1 if s > 0 else 0, s, bufs[stage][1])

    def forward(p, h, stage, s):
        return scatter_copy(4 if s > 0 else 5, p, h, stage, s, 0 if s > 0 else 1, s, bufs[stage][2])

    def f32(v):
        return v.astype(jnp.float32)

    def send_first(p, h, stage):
        for s in both:
            go(far(p, h, stage, s))
        for s in both:
            go(near(p, h, stage, s))

    def send_second(p, h, stage):
        for s in both:
            far(p, h, stage, s).wait_recv()
            side = 0 if s > 0 else 1
            at = (*dest(h, stage, s), slice(None), columns(p, side))
            parts[at] = (f32(parts[at]) + f32(bufs[stage][0][p, h, side])).astype(jnp.bfloat16)
            go(forward(p, h, stage, s))

    def sum_own(p, h, stage):
        for s in both:
            near(p, h, stage, s).wait_recv()
        for side, s in enumerate(both):
            forward(p, h, stage, s).wait_recv()
            cols = columns(p, side)
            at = (*dest(h, stage, 0), slice(None), cols)
            total = f32(parts[at]) + f32(bufs[stage][1][p, h, 1 - side]) + f32(bufs[stage][2][p, h, side])
            if stage == 0:
                parts[at] = total.astype(jnp.bfloat16)
            else:
                mine = pl.ds(h * HALF, HALF)
                tok[mine, cols] = (residual[mine, cols] + total).astype(jnp.bfloat16)

    for p in range(PIECES):
        down_piece(p)
        for h in range(2):
            send_first(p, h, 0)
    feed(9)
    for p in range(PIECES):
        for h in range(2):
            send_second(p, h, 0)
    feed(10)
    for p in range(PIECES):
        for h in range(2):
            sum_own(p, h, 0)
            send_first(p, h, 1)
    feed(11)
    for p in range(PIECES):
        for h in range(2):
            send_second(p, h, 1)
    feed(12)
    for p in range(PIECES):
        for h in range(2):
            sum_own(p, h, 1)
    result = pltpu.make_async_copy(tok, out_ref, load_sem.at[0])
    result.start()

    stay.wait()
    for point, amount in enumerate(FEED):
        if amount:
            together = slots_copy(amount, mig_send.at[point], mig_recv.at[point])
            together.wait_send()
            together.wait_recv()
    slots_copy(len(PEERS) * PER_PEER, ag_send, mig_local).wait_send()
    slots_copy(len(PEERS) * PER_PEER, rs_send, mig_local).wait_send()
    result.wait()


def layer(tokens, queries, fresh_kv, old_cache, old_slot, new_owner, lengths, gain, gate_weight, up_weight, down_weight):
    rows, width = tokens.shape
    share = gate_weight.shape[1]
    _, cache_len, kv_width = old_cache.shape
    slots = SIDE * SIDE * PER_PEER
    mid = width // PIECES // 2
    bf16 = jnp.bfloat16
    return pl.pallas_call(
        layer_kernel,
        name="layer",
        out_shape=[
            pltpu.VMEM((slots, cache_len, kv_width), bf16),
            pltpu.VMEM((rows, width), bf16),
        ],
        in_specs=[ANY] * 11,
        out_specs=[ANY, ANY],
        scratch_shapes=[
            pltpu.SMEM((rows,), jnp.int32),
            pltpu.SMEM((rows,), jnp.int32),
            pltpu.SMEM((rows,), jnp.int32),
            pltpu.VMEM((8, 128), jnp.int32),
            pltpu.SMEM((8, 128), jnp.int32),
            pltpu.VMEM((rows, width), bf16),
            pltpu.VMEM((rows, width), bf16),
            pltpu.VMEM(fresh_kv.shape, bf16),
            pltpu.VMEM(old_cache.shape, bf16),
            pltpu.VMEM((width,), bf16),
            pltpu.VMEM((rows + 1, cache_len, kv_width), bf16),
            pltpu.VMEM((slots, cache_len, kv_width), bf16),
            pltpu.VMEM((share // HD, width, 2 * HD), bf16),
            pltpu.VMEM((share, width), bf16),
            pltpu.VMEM((SIDE, SIDE, 2, HALF, width), bf16),
            pltpu.VMEM((SIDE, SIDE, 2, HALF, width), bf16),
            pltpu.VMEM((SIDE * SIDE * rows, share), bf16),
            pltpu.VMEM((rows, width), jnp.float32),
            pltpu.VMEM((PIECES, 2, 2, SIDE, HALF, mid), bf16),
            pltpu.VMEM((PIECES, 2, 2, SIDE, HALF, mid), bf16),
            pltpu.VMEM((PIECES, 2, 2, SIDE, HALF, mid), bf16),
            pltpu.VMEM((PIECES, 2, 2, HALF, mid), bf16),
            pltpu.VMEM((PIECES, 2, 2, HALF, mid), bf16),
            pltpu.VMEM((PIECES, 2, 2, HALF, mid), bf16),
            pltpu.SemaphoreType.DMA((8,)),
            pltpu.SemaphoreType.DMA((2 * (share // HD) + 1,)),
            pltpu.SemaphoreType.DMA((len(FEED),)),
            pltpu.SemaphoreType.DMA((len(FEED),)),
            pltpu.SemaphoreType.DMA,
            pltpu.SemaphoreType.DMA,
            pltpu.SemaphoreType.DMA((2, 20)),
            pltpu.SemaphoreType.DMA,
            pltpu.SemaphoreType.DMA((PIECES, 2, 2, 6)),
        ],
        compiler_params=pltpu.CompilerParams(
            collective_id=0, has_side_effects=True, vmem_limit_bytes=58 << 20
        ),
    )(
        tokens, queries, fresh_kv, old_cache, old_slot, new_owner, lengths, gain, gate_weight, up_weight, down_weight
    )


def finish_kernel(newc_ref, out_ref, newc_out, out_out, sems):
    copies = (
        pltpu.make_async_copy(newc_ref, newc_out, sems.at[0]),
        pltpu.make_async_copy(out_ref, out_out, sems.at[1]),
    )
    for c in copies:
        c.start()
    for c in copies:
        c.wait()


def finish(newc, out):
    return pl.pallas_call(
        finish_kernel,
        name="finish",
        out_shape=[jax.ShapeDtypeStruct(newc.shape, newc.dtype), jax.ShapeDtypeStruct(out.shape, out.dtype)],
        in_specs=[ANY, ANY],
        out_specs=[ANY, ANY],
        scratch_shapes=[pltpu.SemaphoreType.DMA((2,))],
        compiler_params=pltpu.CompilerParams(vmem_limit_bytes=1 << 20),
    )(newc, out)


def per_device(
    tokens,
    queries,
    fresh_kv,
    old_cache,
    old_slot,
    new_owner,
    lengths,
    norm_gain,
    gate_weight,
    up_weight,
    down_weight,
):
    newc, out = layer(
        tokens, queries, fresh_kv, old_cache, old_slot, new_owner.reshape(-1), lengths, norm_gain,
        gate_weight, up_weight, down_weight,
    )
    new_cache, layer_out = finish(newc, out)
    return (layer_out, new_cache)


def solution(mesh):
    placed = (
        P(("rep", "grp"), None),
        P(("rep", "grp"), None),
        P(("rep", "grp"), None),
        P(("rep", "grp"), None, None),
        P(("rep", "grp")),
        P(("rep", "grp"), None),
        P(("rep", "grp")),
        P("rep"),
        P("rep", "grp"),
        P("rep", "grp"),
        P(("rep", "grp"), None),
    )
    return jax.shard_map(
        per_device,
        mesh=mesh,
        in_specs=placed,
        out_specs=(P(("rep", "grp"), None), P(("rep", "grp"), None, None)),
        check_vma=False,
    )
```

```python
import jax
import jax.numpy as jnp
from jax import lax
from jax.experimental import pallas as pl
from jax.experimental.pallas import tpu as pltpu
from jax.sharding import PartitionSpec as P

FEED = (20, 0, 0, 0, 0, 0, 0, 3, 20, 0, 8, 6, 3)
PIECES = 2
KVH = 4
HD = 128
PER_PEER = 4
SIDE = 4
HALF = 16
MESH = pl.DeviceIdType.MESH
ANY = pl.BlockSpec(memory_space=pl.ANY)
PEERS = (
    (2, 2), (1, 0), (0, 1), (3, 0), (0, 3), (2, 1), (1, 2), (2, 3),
    (3, 2), (2, 0), (0, 2), (1, 1), (3, 3), (1, 3), (3, 1),
)


def layer_kernel(tok_hbm, q_hbm, fresh_hbm, cache_hbm, slot_hbm, owner_hbm, len_hbm, gain_hbm,
                 gate_hbm, up_hbm, down_hbm,
                 newc_ref, out_ref,
                 slot_at, owner_at, len_at, table, table_at,
                 tok, query, fresh, cache, gain, upd, send, w_in, w_down, full, parts, hidden, residual,
                 r1in, r1own, r1fwd, r2in, r2own, r2fwd,
                 load_sem, w_sem, mig_send, mig_recv, mig_local,
                 ag_send, ag_recv, rs_send, rs_recv):
    rows, width = tok.shape
    mid = width // 2
    left, right = pl.ds(0, mid), pl.ds(mid, mid)
    grp, rep = lax.axis_index("grp"), lax.axis_index("rep")
    x, y = grp // SIDE, grp % SIDE

    def device(px, py):
        return ((px + SIDE) % SIDE * SIDE + (py + SIDE) % SIDE, rep)

    barrier = pltpu.get_barrier_semaphore()
    for dx, dy in PEERS:
        pl.semaphore_signal(barrier, inc=1, device_id=device(x + dx, y + dy), device_id_type=MESH)
    pairs = (
        (slot_hbm, slot_at), (owner_hbm, owner_at), (len_hbm, len_at), (cache_hbm, cache), (fresh_hbm, fresh),
        (q_hbm, query), (tok_hbm, tok), (gain_hbm, gain),
    )
    loads = [pltpu.make_async_copy(src, dst, load_sem.at[i]) for i, (src, dst) in enumerate(pairs)]
    for c in loads:
        c.start()

    cache_len, kv_width = cache.shape[1], cache.shape[2]
    for c in loads[:3]:
        c.wait()
    lane = lax.broadcasted_iota(jnp.int32, (rows, 128), 1)
    sub = lax.broadcasted_iota(jnp.int32, (rows, 128), 0)
    owner_row = jnp.full((rows, 128), -1, jnp.int32)
    owner_col = jnp.zeros((rows, 128), jnp.int32)
    for r in range(rows):
        owner_row = jnp.where(lane == r, owner_at[r], owner_row)
        owner_col = jnp.where(sub == r, owner_at[r], owner_col)
    before = (owner_row == owner_col) & (lane < sub)
    rank = jnp.sum(before.astype(jnp.int32), axis=1, keepdims=True)
    fills = (owner_col * PER_PEER + rank == lane).astype(jnp.int32)
    table[...] = jnp.broadcast_to(rows + jnp.sum(fills * (sub - rows), axis=0, keepdims=True), table.shape)
    to_smem = pltpu.make_async_copy(table, table_at, load_sem.at[0])
    to_smem.start()

    for c in loads[3:5]:
        c.wait()
    position = lax.broadcasted_iota(jnp.int32, (cache_len, kv_width), 0)

    for r in range(rows):
        new = jnp.broadcast_to(fresh[r : r + 1, :].astype(jnp.float32), position.shape)
        old = cache[slot_at[r]].astype(jnp.float32)
        upd[r] = jnp.where(position == len_at[r], new, old).astype(upd.dtype)
    upd[rows] = jnp.zeros((cache_len, kv_width), upd.dtype)
    to_smem.wait()
    for k in range(PER_PEER):
        for m in range(SIDE * SIDE):
            send[m * PER_PEER + k] = upd[table_at[0, m * PER_PEER + k]]
    pl.semaphore_wait(barrier, len(PEERS))

    def slots_copy(amount, send_sem, recv_sem):
        return pltpu.make_async_remote_copy(
            src_ref=send.at[pl.ds(0, amount)], dst_ref=newc_ref.at[pl.ds(0, amount)],
            send_sem=send_sem, recv_sem=recv_sem, device_id=device(x + 1, y), device_id_type=MESH,
        )

    def migrate(i, k, group):
        dx, dy = PEERS[i]
        target = device(x + dx, y + dy)
        return pltpu.make_async_remote_copy(
            src_ref=send.at[target[0] * PER_PEER + k],
            dst_ref=newc_ref.at[grp * PER_PEER + k],
            send_sem=mig_send.at[group],
            recv_sem=mig_recv.at[group],
            device_id=target,
            device_id_type=MESH,
        )

    queue = [(i, k) for k in range(PER_PEER) for i in range(len(PEERS))]

    def feed(point):
        for _ in range(FEED[point]):
            migrate(*queue.pop(0), point).start()

    own_slots = pl.ds(grp * PER_PEER, PER_PEER)
    stay = pltpu.make_async_copy(send.at[own_slots], newc_ref.at[own_slots], mig_local)
    feed(0)
    stay.start()

    tiles = w_in.shape[0]
    w_copies = []
    for j in range(tiles):
        cols = pl.ds(j * HD, HD)
        w_copies.append(pltpu.make_async_copy(gate_hbm.at[:, cols], w_in.at[j, :, pl.ds(0, HD)], w_sem.at[2 * j]))
        w_copies.append(pltpu.make_async_copy(up_hbm.at[:, cols], w_in.at[j, :, pl.ds(HD, HD)], w_sem.at[2 * j + 1]))
    w_copies.append(pltpu.make_async_copy(down_hbm, w_down, w_sem.at[2 * tiles]))
    for c in w_copies:
        c.start()
    for c in loads[5:]:
        c.wait()

    cols_n = rows * cache_len
    row_of = lax.broadcasted_iota(jnp.int32, (rows, cols_n), 0)
    col_of = lax.broadcasted_iota(jnp.int32, (rows, cols_n), 1)
    length = jnp.zeros((8, cols_n), jnp.int32)
    request = lax.broadcasted_iota(jnp.int32, (8, cols_n), 1) // cache_len
    for r in range(rows):
        length = jnp.where(request == r, len_at[r], length)
    length = jnp.concatenate([length] * (rows // 8), axis=0)
    valid = (col_of // cache_len == row_of) & (col_of % cache_len <= length)
    bias = jnp.where(valid, 0.0, -1e30).astype(jnp.float32)
    heads_per = width // HD // KVH
    bias = jnp.concatenate([bias] * heads_per, axis=0)
    for g in range(KVH):
        keys = upd[:rows, :, g * HD : (g + 1) * HD].reshape(cols_n, HD)
        values = upd[:rows, :, (KVH + g) * HD : (KVH + g + 1) * HD].reshape(cols_n, HD)
        heads = [query[:, (g * heads_per + h) * HD : (g * heads_per + h + 1) * HD] for h in range(heads_per)]
        scores = lax.dot_general(
            jnp.concatenate(heads, axis=0), keys, (((1,), (1,)), ((), ())), preferred_element_type=jnp.float32
        )
        scores = scores * (HD**-0.5) + bias
        expd = jnp.exp(scores - jnp.max(scores, axis=1, keepdims=True))
        weights = (expd * (1.0 / jnp.sum(expd, axis=1, keepdims=True))).astype(jnp.bfloat16)
        attended = jnp.dot(weights, values, preferred_element_type=jnp.float32).astype(jnp.bfloat16)
        for h in range(heads_per):
            at = slice((g * heads_per + h) * HD, (g * heads_per + h + 1) * HD)
            residual[:, at] = attended[h * rows : (h + 1) * rows].astype(jnp.float32) + tok[:, at].astype(jnp.float32)
    res = residual[...]
    meansq = jnp.mean(res * res, axis=1, keepdims=True)
    normed = (res * lax.rsqrt(meansq + 1e-05) * gain[...].astype(jnp.float32).reshape(1, width)).astype(jnp.bfloat16)
    full[x, y] = normed.reshape(2, HALF, width)

    def peer(h, da, db):
        return device(x + da, y + db) if h == 0 else device(x + db, y + da)

    def block(h, da, db):
        px, py = (da, db) if h == 0 else (db, da)
        return ((x + px + SIDE) % SIDE, (y + py + SIDE) % SIDE, h)

    def gather_copy(n, h, da, db, cols, ta, tb):
        ref = full.at[(*block(h, da, db), slice(None), cols)]
        return pltpu.make_async_remote_copy(
            src_ref=ref, dst_ref=ref, send_sem=ag_send, recv_sem=ag_recv.at[h, n],
            device_id=peer(h, ta, tb), device_id_type=MESH,
        )

    everything = pl.ds(0, width)
    def go(copy):
        copy.start()

    ORIGINS = (0, -1, 1, 2)

    def first(h, s):
        return gather_copy(0 if s > 0 else 1, h, 0, 0, everything, s, 0)

    def first_forward(h, s):
        return gather_copy(2 if s > 0 else 3, h, -s, 0, left if s > 0 else right, s, 0)

    def second(h, i, s):
        return gather_copy(4 + 2 * i + (s < 0), h, ORIGINS[i], 0, everything, 0, s)

    def second_forward(h, i, s):
        return gather_copy(12 + 2 * i + (s < 0), h, ORIGINS[i], -s, left if s > 0 else right, 0, s)

    both = (1, -1)
    for h in range(2):
        for s in both:
            go(first(h, s))
    for h in range(2):
        for s in both:
            go(second(h, 0, s))
    feed(1)
    for i, s in ((1, 1), (2, -1)):
        for h in range(2):
            first(h, s).wait_recv()
            go(first_forward(h, s))
            for t in both:
                go(second(h, i, t))
    feed(2)
    for h in range(2):
        for s in both:
            second(h, 0, s).wait_recv()
            go(second_forward(h, 0, s))
    feed(3)
    for h in range(2):
        for s in both:
            first_forward(h, s).wait_recv()
        for t in both:
            go(second(h, 3, t))
    for i in (1, 2, 3):
        feed(3 + i)
        for h in range(2):
            for s in both:
                second(h, i, s).wait_recv()
                go(second_forward(h, i, s))
    feed(7)
    for i in range(4):
        for h in range(2):
            for s in both:
                second_forward(h, i, s).wait_recv()

    feed(8)
    for c in w_copies:
        c.wait()
    all_rows = SIDE * SIDE * rows

    def up_tile(j, carry):
        pre = jnp.dot(full[...].reshape(all_rows, width), w_in[j], preferred_element_type=jnp.float32)
        gate_pre, up_pre = pre[:, :HD], pre[:, HD:]
        act = gate_pre / (1.0 + jnp.exp(-gate_pre)) * up_pre
        hidden[:, pl.ds(pl.multiple_of(j * HD, HD), HD)] = act.astype(jnp.bfloat16)
        return carry

    lax.fori_loop(0, tiles, up_tile, 0)
    step = 2 * HD
    piece_width = width // PIECES
    half_width = piece_width // 2

    def down_piece(p):
        def down_tile(n, carry):
            cols = pl.ds(pl.multiple_of(n * step, step), step)
            part = jnp.dot(hidden[...], w_down[:, cols], preferred_element_type=jnp.float32)
            parts[:, :, :, :, cols] = part.astype(jnp.bfloat16).reshape(SIDE, SIDE, 2, HALF, step)
            return carry

        lax.fori_loop(p * piece_width // step, (p + 1) * piece_width // step, down_tile, 0)

    def dest(h, stage, d):
        if stage == 0:
            b = ((y if h == 0 else x) + d + SIDE) % SIDE
            return (slice(None), b, h) if h == 0 else (b, slice(None), h)
        return block(h, d, 0)

    def columns(p, side):
        return pl.ds(p * piece_width + side * half_width, half_width)

    def scatter_copy(n, p, h, stage, d, side, s, buf):
        return pltpu.make_async_remote_copy(
            src_ref=parts.at[(*dest(h, stage, d), slice(None), columns(p, side))],
            dst_ref=buf.at[p, h, 0 if s > 0 else 1],
            send_sem=rs_send, recv_sem=rs_recv.at[p, h, stage, n],
            device_id=peer(h, 0, s) if stage == 0 else peer(h, s, 0), device_id_type=MESH,
        )

    bufs = ((r1in, r1own, r1fwd), (r2in, r2own, r2fwd))

    def far(p, h, stage, s):
        return scatter_copy(0 if s > 0 else 1, p, h, stage, 2, 0 if s > 0 else 1, s, bufs[stage][0])

    def near(p, h, stage, s):
        return scatter_copy(2 if s > 0 else 3, p, h, stage, s, 1 if s > 0 else 0, s, bufs[stage][1])

    def forward(p, h, stage, s):
        return scatter_copy(4 if s > 0 else 5, p, h, stage, s, 0 if s > 0 else 1, s, bufs[stage][2])

    def f32(v):
        return v.astype(jnp.float32)

    def send_first(p, h, stage):
        for s in both:
            go(far(p, h, stage, s))
        for s in both:
            go(near(p, h, stage, s))

    def send_second(p, h, stage):
        for s in both:
            far(p, h, stage, s).wait_recv()
            side = 0 if s > 0 else 1
            at = (*dest(h, stage, s), slice(None), columns(p, side))
            parts[at] = (f32(parts[at]) + f32(bufs[stage][0][p, h, side])).astype(jnp.bfloat16)
            go(forward(p, h, stage, s))

    def sum_own(p, h, stage):
        for s in both:
            near(p, h, stage, s).wait_recv()
        for side, s in enumerate(both):
            forward(p, h, stage, s).wait_recv()
            cols = columns(p, side)
            at = (*dest(h, stage, 0), slice(None), cols)
            total = f32(parts[at]) + f32(bufs[stage][1][p, h, 1 - side]) + f32(bufs[stage][2][p, h, side])
            if stage == 0:
                parts[at] = total.astype(jnp.bfloat16)
            else:
                mine = pl.ds(h * HALF, HALF)
                tok[mine, cols] = (residual[mine, cols] + total).astype(jnp.bfloat16)

    for p in range(PIECES):
        down_piece(p)
        for h in range(2):
            send_first(p, h, 0)
    feed(9)
    for p in range(PIECES):
        for h in range(2):
            send_second(p, h, 0)
    feed(10)
    for p in range(PIECES):
        for h in range(2):
            sum_own(p, h, 0)
            send_first(p, h, 1)
    feed(11)
    for p in range(PIECES):
        for h in range(2):
            send_second(p, h, 1)
    feed(12)
    for p in range(PIECES):
        for h in range(2):
            sum_own(p, h, 1)
    result = pltpu.make_async_copy(tok, out_ref, load_sem.at[0])
    result.start()

    stay.wait()
    for point, amount in enumerate(FEED):
        if amount:
            together = slots_copy(amount, mig_send.at[point], mig_recv.at[point])
            together.wait_send()
            together.wait_recv()
    slots_copy(len(PEERS) * PER_PEER, ag_send, mig_local).wait_send()
    slots_copy(len(PEERS) * PER_PEER, rs_send, mig_local).wait_send()
    result.wait()


def layer(tokens, queries, fresh_kv, old_cache, old_slot, new_owner, lengths, gain, gate_weight, up_weight, down_weight):
    rows, width = tokens.shape
    share = gate_weight.shape[1]
    _, cache_len, kv_width = old_cache.shape
    slots = SIDE * SIDE * PER_PEER
    mid = width // PIECES // 2
    bf16 = jnp.bfloat16
    return pl.pallas_call(
        layer_kernel,
        name="layer",
        out_shape=[
            pltpu.VMEM((slots, cache_len, kv_width), bf16),
            pltpu.VMEM((rows, width), bf16),
        ],
        in_specs=[ANY] * 11,
        out_specs=[ANY, ANY],
        scratch_shapes=[
            pltpu.SMEM((rows,), jnp.int32),
            pltpu.SMEM((rows,), jnp.int32),
            pltpu.SMEM((rows,), jnp.int32),
            pltpu.VMEM((8, 128), jnp.int32),
            pltpu.SMEM((8, 128), jnp.int32),
            pltpu.VMEM((rows, width), bf16),
            pltpu.VMEM((rows, width), bf16),
            pltpu.VMEM(fresh_kv.shape, bf16),
            pltpu.VMEM(old_cache.shape, bf16),
            pltpu.VMEM((width,), bf16),
            pltpu.VMEM((rows + 1, cache_len, kv_width), bf16),
            pltpu.VMEM((slots, cache_len, kv_width), bf16),
            pltpu.VMEM((share // HD, width, 2 * HD), bf16),
            pltpu.VMEM((share, width), bf16),
            pltpu.VMEM((SIDE, SIDE, 2, HALF, width), bf16),
            pltpu.VMEM((SIDE, SIDE, 2, HALF, width), bf16),
            pltpu.VMEM((SIDE * SIDE * rows, share), bf16),
            pltpu.VMEM((rows, width), jnp.float32),
            pltpu.VMEM((PIECES, 2, 2, SIDE, HALF, mid), bf16),
            pltpu.VMEM((PIECES, 2, 2, SIDE, HALF, mid), bf16),
            pltpu.VMEM((PIECES, 2, 2, SIDE, HALF, mid), bf16),
            pltpu.VMEM((PIECES, 2, 2, HALF, mid), bf16),
            pltpu.VMEM((PIECES, 2, 2, HALF, mid), bf16),
            pltpu.VMEM((PIECES, 2, 2, HALF, mid), bf16),
            pltpu.SemaphoreType.DMA((8,)),
            pltpu.SemaphoreType.DMA((2 * (share // HD) + 1,)),
            pltpu.SemaphoreType.DMA((len(FEED),)),
            pltpu.SemaphoreType.DMA((len(FEED),)),
            pltpu.SemaphoreType.DMA,
            pltpu.SemaphoreType.DMA,
            pltpu.SemaphoreType.DMA((2, 20)),
            pltpu.SemaphoreType.DMA,
            pltpu.SemaphoreType.DMA((PIECES, 2, 2, 6)),
        ],
        compiler_params=pltpu.CompilerParams(
            collective_id=0, has_side_effects=True, vmem_limit_bytes=58 << 20
        ),
    )(
        tokens, queries, fresh_kv, old_cache, old_slot, new_owner, lengths, gain, gate_weight, up_weight, down_weight
    )


def finish_kernel(newc_ref, out_ref, newc_out, out_out, sems):
    copies = (
        pltpu.make_async_copy(newc_ref, newc_out, sems.at[0]),
        pltpu.make_async_copy(out_ref, out_out, sems.at[1]),
    )
    for c in copies:
        c.start()
    for c in copies:
        c.wait()


def finish(newc, out):
    return pl.pallas_call(
        finish_kernel,
        name="finish",
        out_shape=[jax.ShapeDtypeStruct(newc.shape, newc.dtype), jax.ShapeDtypeStruct(out.shape, out.dtype)],
        in_specs=[ANY, ANY],
        out_specs=[ANY, ANY],
        scratch_shapes=[pltpu.SemaphoreType.DMA((2,))],
        compiler_params=pltpu.CompilerParams(vmem_limit_bytes=1 << 20),
    )(newc, out)


def per_device(
    tokens,
    queries,
    fresh_kv,
    old_cache,
    old_slot,
    new_owner,
    lengths,
    norm_gain,
    gate_weight,
    up_weight,
    down_weight,
):
    newc, out = layer(
        tokens, queries, fresh_kv, old_cache, old_slot, new_owner.reshape(-1), lengths, norm_gain,
        gate_weight, up_weight, down_weight,
    )
    new_cache, layer_out = finish(newc, out)
    return (layer_out, new_cache)


def solution(mesh):
    placed = (
        P(("rep", "grp"), None),
        P(("rep", "grp"), None),
        P(("rep", "grp"), None),
        P(("rep", "grp"), None, None),
        P(("rep", "grp")),
        P(("rep", "grp"), None),
        P(("rep", "grp")),
        P("rep"),
        P("rep", "grp"),
        P("rep", "grp"),
        P(("rep", "grp"), None),
    )
    return jax.shard_map(
        per_device,
        mesh=mesh,
        in_specs=placed,
        out_specs=(P(("rep", "grp"), None), P(("rep", "grp"), None, None)),
        check_vma=False,
    )
```

```python
import jax
import jax.numpy as jnp
from jax import lax
from jax.experimental import pallas as pl
from jax.experimental.pallas import tpu as pltpu
from jax.sharding import PartitionSpec as P

FEED = (20, 0, 0, 0, 0, 0, 0, 3, 20, 0, 8, 6, 3)
PIECES = 2
KVH = 4
HD = 128
PER_PEER = 4
SIDE = 4
HALF = 16
MESH = pl.DeviceIdType.MESH
ANY = pl.BlockSpec(memory_space=pl.ANY)
PEERS = (
    (2, 2), (1, 0), (0, 1), (3, 0), (0, 3), (2, 1), (1, 2), (2, 3),
    (3, 2), (2, 0), (0, 2), (1, 1), (3, 3), (1, 3), (3, 1),
)


def layer_kernel(tok_hbm, q_hbm, fresh_hbm, cache_hbm, slot_hbm, owner_hbm, len_hbm, gain_hbm,
                 gate_hbm, up_hbm, down_hbm,
                 newc_ref, out_ref,
                 slot_at, owner_at, len_at, table, table_at,
                 tok, query, fresh, cache, gain, upd, send, w_in, w_down, full, parts, hidden, residual,
                 r1in, r1own, r1fwd, r2in, r2own, r2fwd,
                 load_sem, w_sem, mig_send, mig_recv, mig_local,
                 ag_send, ag_recv, rs_send, rs_recv):
    rows, width = tok.shape
    mid = width // 2
    left, right = pl.ds(0, mid), pl.ds(mid, mid)
    grp, rep = lax.axis_index("grp"), lax.axis_index("rep")
    x, y = grp // SIDE, grp % SIDE

    def device(px, py):
        return ((px + SIDE) % SIDE * SIDE + (py + SIDE) % SIDE, rep)

    barrier = pltpu.get_barrier_semaphore()
    for dx, dy in PEERS:
        pl.semaphore_signal(barrier, inc=1, device_id=device(x + dx, y + dy), device_id_type=MESH)
    pairs = (
        (slot_hbm, slot_at), (owner_hbm, owner_at), (len_hbm, len_at), (cache_hbm, cache), (fresh_hbm, fresh),
        (q_hbm, query), (tok_hbm, tok), (gain_hbm, gain),
    )
    loads = [pltpu.make_async_copy(src, dst, load_sem.at[i]) for i, (src, dst) in enumerate(pairs)]
    for c in loads:
        c.start()

    cache_len, kv_width = cache.shape[1], cache.shape[2]
    for c in loads[:3]:
        c.wait()
    lane = lax.broadcasted_iota(jnp.int32, (rows, 128), 1)
    sub = lax.broadcasted_iota(jnp.int32, (rows, 128), 0)
    owner_row = jnp.full((rows, 128), -1, jnp.int32)
    owner_col = jnp.zeros((rows, 128), jnp.int32)
    for r in range(rows):
        owner_row = jnp.where(lane == r, owner_at[r], owner_row)
        owner_col = jnp.where(sub == r, owner_at[r], owner_col)
    before = (owner_row == owner_col) & (lane < sub)
    rank = jnp.sum(before.astype(jnp.int32), axis=1, keepdims=True)
    fills = (owner_col * PER_PEER + rank == lane).astype(jnp.int32)
    table[...] = jnp.broadcast_to(rows + jnp.sum(fills * (sub - rows), axis=0, keepdims=True), table.shape)
    to_smem = pltpu.make_async_copy(table, table_at, load_sem.at[0])
    to_smem.start()

    for c in loads[3:5]:
        c.wait()
    position = lax.broadcasted_iota(jnp.int32, (cache_len, kv_width), 0)

    for r in range(rows):
        new = jnp.broadcast_to(fresh[r : r + 1, :].astype(jnp.float32), position.shape)
        old = cache[slot_at[r]].astype(jnp.float32)
        upd[r] = jnp.where(position == len_at[r], new, old).astype(upd.dtype)
    upd[rows] = jnp.zeros((cache_len, kv_width), upd.dtype)
    to_smem.wait()

    def fill(rounds):
        for k in rounds:
            for m in range(SIDE * SIDE):
                send[m * PER_PEER + k] = upd[table_at[0, m * PER_PEER + k]]

    at_once = -(-FEED[0] // len(PEERS))
    fill(range(at_once))
    pl.semaphore_wait(barrier, len(PEERS))

    def slots_copy(amount, send_sem, recv_sem):
        return pltpu.make_async_remote_copy(
            src_ref=send.at[pl.ds(0, amount)], dst_ref=newc_ref.at[pl.ds(0, amount)],
            send_sem=send_sem, recv_sem=recv_sem, device_id=device(x + 1, y), device_id_type=MESH,
        )

    def migrate(i, k, group):
        dx, dy = PEERS[i]
        target = device(x + dx, y + dy)
        return pltpu.make_async_remote_copy(
            src_ref=send.at[target[0] * PER_PEER + k],
            dst_ref=newc_ref.at[grp * PER_PEER + k],
            send_sem=mig_send.at[group],
            recv_sem=mig_recv.at[group],
            device_id=target,
            device_id_type=MESH,
        )

    queue = [(i, k) for k in range(PER_PEER) for i in range(len(PEERS))]

    def feed(point):
        for _ in range(FEED[point]):
            migrate(*queue.pop(0), point).start()

    own_slots = pl.ds(grp * PER_PEER, PER_PEER)
    stay = pltpu.make_async_copy(send.at[own_slots], newc_ref.at[own_slots], mig_local)
    feed(0)
    fill(range(at_once, PER_PEER))
    stay.start()

    tiles = w_in.shape[0]
    w_copies = []
    for j in range(tiles):
        cols = pl.ds(j * HD, HD)
        w_copies.append(pltpu.make_async_copy(gate_hbm.at[:, cols], w_in.at[j, :, pl.ds(0, HD)], w_sem.at[2 * j]))
        w_copies.append(pltpu.make_async_copy(up_hbm.at[:, cols], w_in.at[j, :, pl.ds(HD, HD)], w_sem.at[2 * j + 1]))
    w_copies.append(pltpu.make_async_copy(down_hbm, w_down, w_sem.at[2 * tiles]))
    for c in w_copies:
        c.start()
    for c in loads[5:]:
        c.wait()

    cols_n = rows * cache_len
    row_of = lax.broadcasted_iota(jnp.int32, (rows, cols_n), 0)
    col_of = lax.broadcasted_iota(jnp.int32, (rows, cols_n), 1)
    length = jnp.zeros((8, cols_n), jnp.int32)
    request = lax.broadcasted_iota(jnp.int32, (8, cols_n), 1) // cache_len
    for r in range(rows):
        length = jnp.where(request == r, len_at[r], length)
    length = jnp.concatenate([length] * (rows // 8), axis=0)
    valid = (col_of // cache_len == row_of) & (col_of % cache_len <= length)
    bias = jnp.where(valid, 0.0, -1e30).astype(jnp.float32)
    heads_per = width // HD // KVH
    bias = jnp.concatenate([bias] * heads_per, axis=0)
    for g in range(KVH):
        keys = upd[:rows, :, g * HD : (g + 1) * HD].reshape(cols_n, HD)
        values = upd[:rows, :, (KVH + g) * HD : (KVH + g + 1) * HD].reshape(cols_n, HD)
        heads = [query[:, (g * heads_per + h) * HD : (g * heads_per + h + 1) * HD] for h in range(heads_per)]
        scores = lax.dot_general(
            jnp.concatenate(heads, axis=0), keys, (((1,), (1,)), ((), ())), preferred_element_type=jnp.float32
        )
        scores = scores * (HD**-0.5) + bias
        expd = jnp.exp(scores - jnp.max(scores, axis=1, keepdims=True))
        weights = (expd * (1.0 / jnp.sum(expd, axis=1, keepdims=True))).astype(jnp.bfloat16)
        attended = jnp.dot(weights, values, preferred_element_type=jnp.float32).astype(jnp.bfloat16)
        for h in range(heads_per):
            at = slice((g * heads_per + h) * HD, (g * heads_per + h + 1) * HD)
            residual[:, at] = attended[h * rows : (h + 1) * rows].astype(jnp.float32) + tok[:, at].astype(jnp.float32)
    res = residual[...]
    meansq = jnp.mean(res * res, axis=1, keepdims=True)
    normed = (res * lax.rsqrt(meansq + 1e-05) * gain[...].astype(jnp.float32).reshape(1, width)).astype(jnp.bfloat16)
    full[x, y] = normed.reshape(2, HALF, width)

    def peer(h, da, db):
        return device(x + da, y + db) if h == 0 else device(x + db, y + da)

    def block(h, da, db):
        px, py = (da, db) if h == 0 else (db, da)
        return ((x + px + SIDE) % SIDE, (y + py + SIDE) % SIDE, h)

    def gather_copy(n, h, da, db, cols, ta, tb):
        ref = full.at[(*block(h, da, db), slice(None), cols)]
        return pltpu.make_async_remote_copy(
            src_ref=ref, dst_ref=ref, send_sem=ag_send, recv_sem=ag_recv.at[h, n],
            device_id=peer(h, ta, tb), device_id_type=MESH,
        )

    everything = pl.ds(0, width)
    def go(copy):
        copy.start()

    ORIGINS = (0, -1, 1, 2)

    def first(h, s):
        return gather_copy(0 if s > 0 else 1, h, 0, 0, everything, s, 0)

    def first_forward(h, s):
        return gather_copy(2 if s > 0 else 3, h, -s, 0, left if s > 0 else right, s, 0)

    def second(h, i, s):
        return gather_copy(4 + 2 * i + (s < 0), h, ORIGINS[i], 0, everything, 0, s)

    def second_forward(h, i, s):
        return gather_copy(12 + 2 * i + (s < 0), h, ORIGINS[i], -s, left if s > 0 else right, 0, s)

    both = (1, -1)
    for h in range(2):
        for s in both:
            go(first(h, s))
    for h in range(2):
        for s in both:
            go(second(h, 0, s))
    feed(1)
    for i, s in ((1, 1), (2, -1)):
        for h in range(2):
            first(h, s).wait_recv()
            go(first_forward(h, s))
            for t in both:
                go(second(h, i, t))
    feed(2)
    for h in range(2):
        for s in both:
            second(h, 0, s).wait_recv()
            go(second_forward(h, 0, s))
    feed(3)
    for h in range(2):
        for s in both:
            first_forward(h, s).wait_recv()
        for t in both:
            go(second(h, 3, t))
    for i in (1, 2, 3):
        feed(3 + i)
        for h in range(2):
            for s in both:
                second(h, i, s).wait_recv()
                go(second_forward(h, i, s))
    feed(7)
    for i in range(4):
        for h in range(2):
            for s in both:
                second_forward(h, i, s).wait_recv()

    feed(8)
    for c in w_copies:
        c.wait()
    all_rows = SIDE * SIDE * rows

    def up_tile(j, carry):
        pre = jnp.dot(full[...].reshape(all_rows, width), w_in[j], preferred_element_type=jnp.float32)
        gate_pre, up_pre = pre[:, :HD], pre[:, HD:]
        act = gate_pre / (1.0 + jnp.exp(-gate_pre)) * up_pre
        hidden[:, pl.ds(pl.multiple_of(j * HD, HD), HD)] = act.astype(jnp.bfloat16)
        return carry

    lax.fori_loop(0, tiles, up_tile, 0)
    step = 2 * HD
    piece_width = width // PIECES
    half_width = piece_width // 2

    def down_piece(p):
        def down_tile(n, carry):
            cols = pl.ds(pl.multiple_of(n * step, step), step)
            part = jnp.dot(hidden[...], w_down[:, cols], preferred_element_type=jnp.float32)
            parts[:, :, :, :, cols] = part.astype(jnp.bfloat16).reshape(SIDE, SIDE, 2, HALF, step)
            return carry

        lax.fori_loop(p * piece_width // step, (p + 1) * piece_width // step, down_tile, 0)

    def dest(h, stage, d):
        if stage == 0:
            b = ((y if h == 0 else x) + d + SIDE) % SIDE
            return (slice(None), b, h) if h == 0 else (b, slice(None), h)
        return block(h, d, 0)

    def columns(p, side):
        return pl.ds(p * piece_width + side * half_width, half_width)

    def scatter_copy(n, p, h, stage, d, side, s, buf):
        return pltpu.make_async_remote_copy(
            src_ref=parts.at[(*dest(h, stage, d), slice(None), columns(p, side))],
            dst_ref=buf.at[p, h, 0 if s > 0 else 1],
            send_sem=rs_send, recv_sem=rs_recv.at[p, h, stage, n],
            device_id=peer(h, 0, s) if stage == 0 else peer(h, s, 0), device_id_type=MESH,
        )

    bufs = ((r1in, r1own, r1fwd), (r2in, r2own, r2fwd))

    def far(p, h, stage, s):
        return scatter_copy(0 if s > 0 else 1, p, h, stage, 2, 0 if s > 0 else 1, s, bufs[stage][0])

    def near(p, h, stage, s):
        return scatter_copy(2 if s > 0 else 3, p, h, stage, s, 1 if s > 0 else 0, s, bufs[stage][1])

    def forward(p, h, stage, s):
        return scatter_copy(4 if s > 0 else 5, p, h, stage, s, 0 if s > 0 else 1, s, bufs[stage][2])

    def f32(v):
        return v.astype(jnp.float32)

    def send_first(p, h, stage):
        for s in both:
            go(far(p, h, stage, s))
        for s in both:
            go(near(p, h, stage, s))

    def send_second(p, h, stage):
        for s in both:
            far(p, h, stage, s).wait_recv()
            side = 0 if s > 0 else 1
            at = (*dest(h, stage, s), slice(None), columns(p, side))
            parts[at] = (f32(parts[at]) + f32(bufs[stage][0][p, h, side])).astype(jnp.bfloat16)
            go(forward(p, h, stage, s))

    def sum_own(p, h, stage):
        for s in both:
            near(p, h, stage, s).wait_recv()
        for side, s in enumerate(both):
            forward(p, h, stage, s).wait_recv()
            cols = columns(p, side)
            at = (*dest(h, stage, 0), slice(None), cols)
            total = f32(parts[at]) + f32(bufs[stage][1][p, h, 1 - side]) + f32(bufs[stage][2][p, h, side])
            if stage == 0:
                parts[at] = total.astype(jnp.bfloat16)
            else:
                mine = pl.ds(h * HALF, HALF)
                tok[mine, cols] = (residual[mine, cols] + total).astype(jnp.bfloat16)

    for p in range(PIECES):
        down_piece(p)
        for h in range(2):
            send_first(p, h, 0)
    feed(9)
    for p in range(PIECES):
        for h in range(2):
            send_second(p, h, 0)
    feed(10)
    for p in range(PIECES):
        for h in range(2):
            sum_own(p, h, 0)
            send_first(p, h, 1)
    feed(11)
    for p in range(PIECES):
        for h in range(2):
            send_second(p, h, 1)
    feed(12)
    for p in range(PIECES):
        for h in range(2):
            sum_own(p, h, 1)
    result = pltpu.make_async_copy(tok, out_ref, load_sem.at[0])
    result.start()

    stay.wait()
    for point, amount in enumerate(FEED):
        if amount:
            together = slots_copy(amount, mig_send.at[point], mig_recv.at[point])
            together.wait_send()
            together.wait_recv()
    slots_copy(len(PEERS) * PER_PEER, ag_send, mig_local).wait_send()
    slots_copy(len(PEERS) * PER_PEER, rs_send, mig_local).wait_send()
    result.wait()


def layer(tokens, queries, fresh_kv, old_cache, old_slot, new_owner, lengths, gain, gate_weight, up_weight, down_weight):
    rows, width = tokens.shape
    share = gate_weight.shape[1]
    _, cache_len, kv_width = old_cache.shape
    slots = SIDE * SIDE * PER_PEER
    mid = width // PIECES // 2
    bf16 = jnp.bfloat16
    return pl.pallas_call(
        layer_kernel,
        name="layer",
        out_shape=[
            pltpu.VMEM((slots, cache_len, kv_width), bf16),
            pltpu.VMEM((rows, width), bf16),
        ],
        in_specs=[ANY] * 11,
        out_specs=[ANY, ANY],
        scratch_shapes=[
            pltpu.SMEM((rows,), jnp.int32),
            pltpu.SMEM((rows,), jnp.int32),
            pltpu.SMEM((rows,), jnp.int32),
            pltpu.VMEM((8, 128), jnp.int32),
            pltpu.SMEM((8, 128), jnp.int32),
            pltpu.VMEM((rows, width), bf16),
            pltpu.VMEM((rows, width), bf16),
            pltpu.VMEM(fresh_kv.shape, bf16),
            pltpu.VMEM(old_cache.shape, bf16),
            pltpu.VMEM((width,), bf16),
            pltpu.VMEM((rows + 1, cache_len, kv_width), bf16),
            pltpu.VMEM((slots, cache_len, kv_width), bf16),
            pltpu.VMEM((share // HD, width, 2 * HD), bf16),
            pltpu.VMEM((share, width), bf16),
            pltpu.VMEM((SIDE, SIDE, 2, HALF, width), bf16),
            pltpu.VMEM((SIDE, SIDE, 2, HALF, width), bf16),
            pltpu.VMEM((SIDE * SIDE * rows, share), bf16),
            pltpu.VMEM((rows, width), jnp.float32),
            pltpu.VMEM((PIECES, 2, 2, SIDE, HALF, mid), bf16),
            pltpu.VMEM((PIECES, 2, 2, SIDE, HALF, mid), bf16),
            pltpu.VMEM((PIECES, 2, 2, SIDE, HALF, mid), bf16),
            pltpu.VMEM((PIECES, 2, 2, HALF, mid), bf16),
            pltpu.VMEM((PIECES, 2, 2, HALF, mid), bf16),
            pltpu.VMEM((PIECES, 2, 2, HALF, mid), bf16),
            pltpu.SemaphoreType.DMA((8,)),
            pltpu.SemaphoreType.DMA((2 * (share // HD) + 1,)),
            pltpu.SemaphoreType.DMA((len(FEED),)),
            pltpu.SemaphoreType.DMA((len(FEED),)),
            pltpu.SemaphoreType.DMA,
            pltpu.SemaphoreType.DMA,
            pltpu.SemaphoreType.DMA((2, 20)),
            pltpu.SemaphoreType.DMA,
            pltpu.SemaphoreType.DMA((PIECES, 2, 2, 6)),
        ],
        compiler_params=pltpu.CompilerParams(
            collective_id=0, has_side_effects=True, vmem_limit_bytes=58 << 20
        ),
    )(
        tokens, queries, fresh_kv, old_cache, old_slot, new_owner, lengths, gain, gate_weight, up_weight, down_weight
    )


def finish_kernel(newc_ref, out_ref, newc_out, out_out, sems):
    copies = (
        pltpu.make_async_copy(newc_ref, newc_out, sems.at[0]),
        pltpu.make_async_copy(out_ref, out_out, sems.at[1]),
    )
    for c in copies:
        c.start()
    for c in copies:
        c.wait()


def finish(newc, out):
    return pl.pallas_call(
        finish_kernel,
        name="finish",
        out_shape=[jax.ShapeDtypeStruct(newc.shape, newc.dtype), jax.ShapeDtypeStruct(out.shape, out.dtype)],
        in_specs=[ANY, ANY],
        out_specs=[ANY, ANY],
        scratch_shapes=[pltpu.SemaphoreType.DMA((2,))],
        compiler_params=pltpu.CompilerParams(vmem_limit_bytes=1 << 20),
    )(newc, out)


def per_device(
    tokens,
    queries,
    fresh_kv,
    old_cache,
    old_slot,
    new_owner,
    lengths,
    norm_gain,
    gate_weight,
    up_weight,
    down_weight,
):
    newc, out = layer(
        tokens, queries, fresh_kv, old_cache, old_slot, new_owner.reshape(-1), lengths, norm_gain,
        gate_weight, up_weight, down_weight,
    )
    new_cache, layer_out = finish(newc, out)
    return (layer_out, new_cache)


def solution(mesh):
    placed = (
        P(("rep", "grp"), None),
        P(("rep", "grp"), None),
        P(("rep", "grp"), None),
        P(("rep", "grp"), None, None),
        P(("rep", "grp")),
        P(("rep", "grp"), None),
        P(("rep", "grp")),
        P("rep"),
        P("rep", "grp"),
        P("rep", "grp"),
        P(("rep", "grp"), None),
    )
    return jax.shard_map(
        per_device,
        mesh=mesh,
        in_specs=placed,
        out_specs=(P(("rep", "grp"), None), P(("rep", "grp"), None, None)),
        check_vma=False,
    )
```
